512 devices in a mesh: dp: 16 (over z), ep: 32 (over x, y, core).
Axes of the slice: x: 4, y: 4, z: 16, core: 2. Of those that a mesh axis runs over, the one named last changes fastest.
Arguments:
- tokens: bfloat16 [16, 4096, 2880], P('dp', 'ep'), may hold values from -6 to 6
- expert_ids: int32 [16, 4096, 4], P('dp', 'ep'), may hold values from 0 to 127, as said below
- slot_pos: int32 [16, 4096, 4], P('dp', 'ep'), may hold values from -1 to 4, as said below
- smooth: float32 [4, 2880], replicated, may hold values from 0.25 to 4
- smoothed_weight: bfloat16 [2880, 2, 11520], P('dp', None, 'ep'), may hold values from -0.109375 to 0.109375
- act_grad: bfloat16 [16, 160, 11520], P('dp', None, 'ep'), may hold values from -1.5 to 1.5
Outputs:
- token_grad: bfloat16 [16, 4096, 2880], P('dp', 'ep')
- weight_grad: float32 [2880, 2, 11520], P('dp', None, 'ep')
The draws below stay inside these ranges and needn't reach their ends.
Inputs may be any that keep to these rules, and one draw needn't show every extreme that they name: `expert_ids`: each token names 4 different experts, at most one of them below 4. `slot_pos`: -1 where the named expert is 4 or above; otherwise the slot of the token in that expert's buffer for the 128 tokens of its block, distinct within the buffer. In every draw one expert below 4 has a full buffer from every block.
All inputs are finite; a program needn't handle non-finite values.
Results may differ from the reference program's by a relative error of at most 0.017.
Values may be sent and summed in bfloat16 or wider, within the bound.
A program may use at most 64 MiB of HBM per device.

```python
import math
import jax
import jax.numpy as jnp
from jax import lax

D = 2880
HID = 2880
EXPERTS_ALL = 128
TOPK = 4
TOK_DEV = 128
SPLIT = 8
EXPERTS = 4
HID_DEV = 360
SLOT = 5
LEN = 4096
BATCH = 16
N_EP = 32


def routing_tables(key):
    key = jax.random.fold_in(key, 7)
    blocks = BATCH * N_EP
    others = EXPERTS_ALL - EXPERTS
    keys = jax.random.split(key, 5)
    full_group = jax.random.randint(keys[0], (), 0, EXPERTS)
    counts = jax.random.randint(keys[1], (blocks, EXPERTS), 1, SLOT + 1)
    counts = jnp.where(jnp.arange(EXPERTS)[None, :] == full_group, SLOT, counts).astype(jnp.int32)
    ends = jnp.cumsum(counts, axis=1)
    starts = ends - counts
    order_scores = jax.random.randint(keys[2], (blocks, TOK_DEV), 0, 1 << 20) * TOK_DEV + jnp.arange(TOK_DEV)
    rank = jnp.argsort(jnp.argsort(order_scores, axis=1), axis=1).astype(jnp.int32)
    inside = (rank[:, :, None] >= starts[:, None, :]) & (rank[:, :, None] < ends[:, None, :])
    has_group = jnp.any(inside, axis=2)
    group_of = jnp.sum(jnp.where(inside, jnp.arange(EXPERTS)[None, None, :], 0), axis=2)
    slot_of = rank - jnp.sum(jnp.where(inside, starts[:, None, :], 0), axis=2)
    other_scores = jax.random.randint(keys[3], (blocks, TOK_DEV, others), 0, 1 << 20) * others + jnp.arange(others)
    picked = EXPERTS + jnp.argsort(other_scores, axis=2)[:, :, :TOPK]
    first_id = jnp.where(has_group, group_of, picked[:, :, 0])
    id_table = jnp.concatenate([first_id[:, :, None], picked[:, :, 1:]], axis=2)
    first_slot = jnp.where(has_group, slot_of, -1)
    slot_table = jnp.concatenate([first_slot[:, :, None], jnp.full((blocks, TOK_DEV, TOPK - 1), -1, jnp.int32)], axis=2)
    column_scores = jax.random.randint(keys[4], (blocks, TOK_DEV, TOPK), 0, 1 << 20) * TOPK + jnp.arange(TOPK)
    column_order = jnp.argsort(column_scores, axis=2)
    id_table = jnp.take_along_axis(id_table, column_order, axis=2)
    slot_table = jnp.take_along_axis(slot_table, column_order, axis=2)
    return (id_table.reshape(BATCH, LEN, TOPK).astype(jnp.int32), slot_table.reshape(BATCH, LEN, TOPK).astype(jnp.int32))


def draw_expert_ids(key, part):
    return routing_tables(key)[0]


def draw_slot_pos(key, part):
    return routing_tables(key)[1]


def steps_of(stream_key, shape, cuts, low, largest):
    factor_of, own = 1.0, jax.random.fold_in(stream_key, 6)
    for axis_at, blocks in cuts:
        steps = jnp.exp(jax.random.uniform(jax.random.fold_in(own, axis_at), (blocks,), jnp.float32, low / len(cuts), largest / len(cuts)))
        factor_of = factor_of * jnp.repeat(steps, shape[axis_at] // blocks).reshape([-1 if axis == axis_at else 1 for axis in range(len(shape))])
    return factor_of


def centred(key, extent, spread, reach, cuts=(), kind=jnp.bfloat16):
    array = jax.random.normal(key, extent, jnp.float32) * spread
    if len(cuts) > 0:
        array = steps_of(key, extent, cuts, -0.22, 0.18) * array
    return jnp.clip(array, min=-reach, max=reach).astype(kind)


def setup_inputs(seed: int = 0) -> dict:
    arg_keys = jax.random.split(jax.random.key(seed), 7)
    return {
        "tokens": centred(arg_keys[0], (BATCH, LEN, D), 1.0, 6.0, ((0, 16), (1, 32))),
        "expert_ids": draw_expert_ids(jax.random.fold_in(arg_keys[6], 71), 0),
        "slot_pos": draw_slot_pos(jax.random.fold_in(arg_keys[6], 71), 0),
        "smooth": jnp.clip(jnp.exp(jax.random.uniform(arg_keys[3], (EXPERTS, D), jnp.float32, math.log(0.25), math.log(4.0))), 0.25, 4.0),
        "smoothed_weight": centred(arg_keys[4], (D, 2, EXPERTS * HID), D ** -0.5, 0.109375, ((0, 16), (2, 32))),
        "act_grad": centred(arg_keys[5], (BATCH, N_EP * SLOT, EXPERTS * HID), 0.1, 1.5, ((0, 16), (2, 32))),
    }


swish_alpha = 1.702


def reference(tokens, expert_ids, slot_pos, smooth, smoothed_weight, act_grad):
    rows_all = EXPERTS * N_EP * SLOT
    weight_grad = jnp.zeros((D, 2, EXPERTS * HID), jnp.float32)
    source_block = (jnp.arange(LEN, dtype=jnp.int32) // TOK_DEV)[:, None]
    token_numbers = jnp.broadcast_to(jnp.arange(LEN, dtype=jnp.int32)[:, None], (LEN, TOPK)).reshape(-1)
    results = []
    for sequence in range(BATCH):
        routed = expert_ids[sequence]
        placed = slot_pos[sequence]
        inside = routed < EXPERTS
        flat_row = jnp.where(inside, routed * (N_EP * SLOT) + source_block * SLOT + placed, rows_all).astype(jnp.int32)
        token_index = jnp.full((rows_all + 1,), LEN, jnp.int32).at[flat_row.reshape(-1)].set(token_numbers)
        padded = jnp.concatenate([tokens[sequence], jnp.zeros((1, D), jnp.bfloat16)], axis=0)
        dispatched = padded[token_index[:rows_all]]
        summed_rows = []
        for group in range(EXPERTS):
            block_rows = dispatched[group * N_EP * SLOT:(group + 1) * N_EP * SLOT]
            factor = smooth[group]
            scaled = (block_rows.astype(jnp.float32) / factor).astype(jnp.bfloat16)
            low = group * HID
            high = (group + 1) * HID
            w_gate = smoothed_weight[:, 0, low:high]
            w_up = smoothed_weight[:, 1, low:high]
            gate_pre = jnp.dot(scaled, w_gate, preferred_element_type=jnp.float32)
            up_pre = jnp.dot(scaled, w_up, preferred_element_type=jnp.float32)
            cotangent = act_grad[sequence][:, low:high].astype(jnp.float32)
            sigmoid_gate = jax.nn.sigmoid(swish_alpha * gate_pre)
            grad_up = (cotangent * gate_pre * sigmoid_gate).astype(jnp.bfloat16)
            grad_gate = (cotangent * (up_pre + 1.0) * sigmoid_gate * (1.0 + swish_alpha * gate_pre * (1.0 - sigmoid_gate))).astype(jnp.bfloat16)
            gate_term = lax.optimization_barrier(jnp.dot(scaled.T, grad_gate, preferred_element_type=jnp.float32).astype(jnp.bfloat16))
            up_term = lax.optimization_barrier(jnp.dot(scaled.T, grad_up, preferred_element_type=jnp.float32).astype(jnp.bfloat16))
            weight_grad = weight_grad.at[:, 0, low:high].add(gate_term.astype(jnp.float32))
            weight_grad = weight_grad.at[:, 1, low:high].add(up_term.astype(jnp.float32))
            combined = jnp.zeros((N_EP * SLOT, D), jnp.float32)
            for shard in range(SPLIT):
                first = shard * HID_DEV
                last = (shard + 1) * HID_DEV
                grad_pair = jnp.concatenate([grad_gate[:, first:last], grad_up[:, first:last]], axis=1)
                weight_pair = jnp.concatenate([w_gate[:, first:last], w_up[:, first:last]], axis=1)
                term = jnp.dot(grad_pair, weight_pair.T, preferred_element_type=jnp.float32) / factor
                term = lax.optimization_barrier(term.astype(jnp.bfloat16))
                combined = combined + term.astype(jnp.float32)
            summed_rows.append(combined)
        summed = jnp.concatenate(summed_rows + [jnp.zeros((1, D), jnp.float32)], axis=0)
        token_total = jnp.zeros((LEN, D), jnp.float32)
        for column in range(TOPK):
            token_total = token_total + summed[flat_row[:, column]]
        results.append(token_total.astype(jnp.bfloat16))
    token_grad = jnp.stack(results, axis=0)
    return token_grad, weight_grad
```

```python
import functools

import jax
import jax.numpy as jnp
from jax import lax
from jax.experimental import pallas as pl
from jax.experimental.pallas import tpu as pltpu
from jax.sharding import PartitionSpec as P

MESH = pl.DeviceIdType.MESH
F32 = jnp.float32
BF16 = jnp.bfloat16
ALPHA = 1.702
Z = 16
E = 32
SHARE = 8
SLOT = 5
ROWS = 160
D = 2880
KC = 180
KP = 184
CH = 2 * KP
HID = 360
HP = 384
WIDE = 1024
BLK = 16
THIRDS = ((0, 1024), (1024, 1024), (2048, 832))
SUBS = ((0, 192), (192, 176))


def mm(a, b):
    return jnp.dot(a, b, preferred_element_type=F32)


def mm_nt(a, b):
    return lax.dot_general(a, b, (((1,), (1,)), ((), ())), preferred_element_type=F32)


def mm_tn(a, b):
    return lax.dot_general(a, b, (((0,), (0,)), ((), ())), preferred_element_type=F32)


def kernel(
    w_ref, tok_ref, ids_ref, pos_ref, smooth_ref, act_ref,
    dw_ref, dtok_ref,
    wbuf, tsend, trecv, rows32, d32, sct, fcol, acc, gpair, cbuf, rsend, rrecv, bthird, psend, precv,
    ag_ss, ag_rs, rs_ss, rs_rs, t_ss, t_rs, p_ss, p_rs,
):
    z = lax.axis_index("dp")
    me = lax.axis_index("ep")
    right, left = lax.rem(z + 1, Z), lax.rem(z + Z - 1, Z)
    group = me // SHARE
    sides = (right, left)

    barrier = pltpu.get_barrier_semaphore()
    for side in sides:
        pl.semaphore_signal(barrier, inc=1, device_id={"dp": side}, device_id_type=MESH)

    @pl.loop(1, E)
    def _(k):
        pl.semaphore_signal(
            barrier, inc=1, device_id={"ep": lax.rem(me + k, E)}, device_id_type=MESH
        )

    wbuf[z] = w_ref[...]
    pl.semaphore_wait(barrier, E + 1)

    def ag_copy(s, way, sub):
        owner = lax.rem(z + Z - s, Z) if way == 0 else lax.rem(z + s, Z)
        first, count = SUBS[sub]
        part = wbuf.at[owner, pl.ds(first, count)]
        return pltpu.make_async_remote_copy(
            src_ref=part, dst_ref=part,
            send_sem=ag_ss.at[way, s, sub], recv_sem=ag_rs.at[way, s, sub],
            device_id={"dp": sides[way]}, device_id_type=MESH,
        )

    def ag_recv(s, way, sub):
        owner = lax.rem(z + Z - 1 - s, Z) if way == 0 else lax.rem(z + 1 + s, Z)
        first, count = SUBS[sub]
        part = wbuf.at[owner, pl.ds(first, count)]
        return pltpu.make_async_remote_copy(
            src_ref=part, dst_ref=part,
            send_sem=ag_ss.at[way, s, sub], recv_sem=ag_rs.at[way, s, sub],
            device_id={"dp": sides[way]}, device_id_type=MESH,
        )

    for sub in range(2):
        for way in range(2):
            ag_copy(0, way, sub).start()

    def match_rows(count, shift):
        row = lax.broadcasted_iota(jnp.int32, (count, 128), 0)
        g = row >> shift
        j = row & (BLK - 1)
        slot = (j * 11) >> 5
        third = j - 3 * slot
        hit = jnp.zeros((count, 128), jnp.bool_)
        for k in range(4):
            hit = hit | ((ids_ref[k : k + 1, :] == g) & (pos_ref[k : k + 1, :] == slot))
        return [
            jnp.where(hit & (third == t), 1.0, 0.0).astype(BF16) for t in range(3)
        ]

    sel = match_rows(4 * BLK, 4)
    for t, (first, count) in enumerate(THIRDS):
        rows = mm_nt(sel[t], tok_ref[first : first + count, :])
        if t == 0:
            rows32[...] = rows
        else:
            rows32[:, 0:count] = rows32[:, 0:count] + rows
    for g in range(4):
        tsend[g] = rows32[g * BLK : (g + 1) * BLK, :].astype(BF16)

    def t_copy(peer, block, slot_at, peer_sem):
        return pltpu.make_async_remote_copy(
            src_ref=tsend.at[block], dst_ref=trecv.at[slot_at],
            send_sem=t_ss.at[peer], recv_sem=t_rs.at[peer_sem],
            device_id={"ep": peer}, device_id_type=MESH,
        )

    @pl.loop(1, E)
    def _(k):
        peer = lax.rem(me + k, E)
        t_copy(peer, peer // SHARE, me, me).start()

    trecv[me] = tsend[group]

    def place_rows(t, tall):
        shape = (E * BLK, ROWS) if tall else (ROWS, E * BLK)
        wide = lax.broadcasted_iota(jnp.int32, shape, 0 if tall else 1)
        r = lax.broadcasted_iota(jnp.int32, shape, 1 if tall else 0)
        s = (r * 205) >> 10
        return jnp.where(wide == s * BLK + (r - SLOT * s) * 3 + t, 1.0, 0.0).astype(BF16)

    def t_wait():
        @pl.loop(1, E)
        def _(k):
            peer = lax.rem(me + E - k, E)
            t_copy(peer, 0, peer, peer).wait_recv()

    def factors():
        row = smooth_ref[pl.ds(group, 1), :]
        for first, count in THIRDS:
            piece = jnp.broadcast_to(row[:, first : first + count], (8, count))
            fcol[first : first + count, :] = piece.T
        fcol[D : D + 64, :] = jnp.ones((64, 8), F32)
        gpair[...] = jnp.zeros_like(gpair)
        acc[...] = jnp.zeros_like(acc)

    def dispatch(t):
        first, count = THIRDS[t]
        wide = trecv[...].reshape(E * BLK, WIDE)
        rows = mm(place_rows(t, False), wide[:, 0:count])
        factor = smooth_ref[pl.ds(group, 1), first : first + count]
        scaled = (rows / factor).astype(BF16).astype(F32)
        d32[first : first + count, :] = scaled.T
        if t == 2:
            d32[D : D + 64, :] = jnp.zeros((64, ROWS), F32)

    def chunks(low, high):
        for o in range(low, high):
            sct[o] = d32[KC * o : KC * o + KP, :].astype(BF16)

    def forward(o):
        left_side = sct[o]
        acc[0] = acc[0] + mm_tn(left_side, wbuf[o, 0:KP])
        acc[1] = acc[1] + mm_tn(left_side, wbuf[o, KP:CH])

    def forward_span(low, high):
        @pl.loop(low, high)
        def _(k):
            forward(lax.rem(z + Z + k, Z))

    ag_tasks = {
        (1, 0): factors,
        (3, 0): lambda: (t_wait(), dispatch(0)),
        (3, 1): lambda: dispatch(1),
        (4, 0): lambda: dispatch(2),
        (4, 1): lambda: chunks(0, 8),
        (5, 0): lambda: chunks(8, 16),
        (5, 1): lambda: forward_span(-2, 3),
        (6, 0): lambda: (forward_span(-5, -2), forward_span(3, 6)),
        (7, 0): lambda: (forward_span(-6, -5), forward_span(6, 7)),
        (7, 1): lambda: (forward_span(-7, -6), forward_span(7, 8)),
    }
    for s in range(1, 8):
        for sub in range(2):
            for way in range(2):
                ag_recv(s - 1, way, sub).wait_recv()
                if s < 7 or way == sub:
                    ag_copy(s, way, sub).start()
            ag_tasks.get((s, sub), lambda: None)()
    ag_recv(7, 0, 0).wait_recv()
    ag_recv(7, 1, 1).wait_recv()
    forward(lax.rem(z + 8, Z))

    gate = acc[0, :, 0:HID]
    up = acc[1, :, 0:HID]
    c = act_ref[...].astype(F32)
    q = 1.0 / (1.0 + jnp.exp(-ALPHA * gate))
    gpair[0, :, 0:HID] = (c * (up + 1.0) * q * (1.0 + ALPHA * gate * (1.0 - q))).astype(BF16)
    gpair[1, :, 0:HID] = (c * gate * q).astype(BF16)

    def term(o, at):
        left_side = sct[o]
        cbuf[at, 0:KP] = mm(left_side, gpair[0])
        cbuf[at, KP:CH] = mm(left_side, gpair[1])

    def rs_copy(t, way, sub):
        first, count = SUBS[sub]
        return pltpu.make_async_remote_copy(
            src_ref=rsend.at[way, t, pl.ds(first, count)],
            dst_ref=rrecv.at[way, t, pl.ds(first, count)],
            send_sem=rs_ss.at[way, t, sub], recv_sem=rs_rs.at[way, t, sub],
            device_id={"dp": sides[way]}, device_id_type=MESH,
        )

    term(lax.rem(z + 8, Z), 0)
    for way in range(2):
        first, count = SUBS[way]
        rsend[way, 0, first : first + count] = cbuf[0, first : first + count].astype(BF16)
        rs_copy(0, way, way).start()

    def back(low, high):
        for o in range(low, high):
            part = mm_nt(wbuf[o, 0:KP], gpair[0]) + mm_nt(wbuf[o, KP:CH], gpair[1])
            d32[KC * o : KC * o + KP, :] = part

    def unscale():
        for first, count in THIRDS:
            bthird[first : first + count, :] = (
                d32[first : first + count, :] / fcol[first : first + count, 0:1]
            ).astype(BF16)
        bthird[D : 3 * WIDE, :] = jnp.zeros((3 * WIDE - D, ROWS), BF16)

    def expand():
        total = None
        for t in range(3):
            rows = mm_nt(place_rows(t, True), bthird[WIDE * t : WIDE * (t + 1), :])
            total = rows if total is None else total + rows
        psend[...] = total.astype(BF16).reshape(E, BLK, WIDE)

    def p_copy(peer, block, slot_at, peer_sem):
        return pltpu.make_async_remote_copy(
            src_ref=psend.at[block], dst_ref=precv.at[slot_at],
            send_sem=p_ss.at[peer], recv_sem=p_rs.at[peer_sem],
            device_id={"ep": peer}, device_id_type=MESH,
        )

    def p_start():
        @pl.loop(1, E)
        def _(k):
            peer = lax.rem(me + k, E)
            p_copy(peer, peer, me, me).start()

        precv[me] = psend[me]

    def p_wait():
        @pl.loop(1, E)
        def _(k):
            peer = lax.rem(me + E - k, E)
            p_copy(peer, 0, peer, peer).wait_recv()

    def combine():
        flat = precv[...].reshape(E * BLK, WIDE)
        pick = match_rows(E * BLK, 7)
        for t, (first, count) in enumerate(THIRDS):
            dtok_ref[first : first + count, :] = mm_tn(flat[:, 0:count], pick[t]).astype(BF16)

    rs_tasks = {
        (1, 0): lambda: back(0, 8),
        (1, 1): lambda: back(8, 16),
        (2, 0): unscale,
        (2, 1): lambda: (expand(), p_start()),
        (6, 0): lambda: (p_wait(), combine()),
    }
    for t in range(1, 8):
        term(lax.rem(z + 8 - t + Z, Z), 0)
        term(lax.rem(z + 8 + t, Z), 1)
        for sub in range(2):
            first, count = SUBS[sub]
            for way in range(2):
                value = cbuf[way, first : first + count]
                if t > 1 or sub == way:
                    rs_copy(t - 1, way, sub).wait_recv()
                    value = value + rrecv[way, t - 1, first : first + count].astype(F32)
                rsend[way, t, first : first + count] = value.astype(BF16)
                rs_copy(t, way, sub).start()
            rs_tasks.get((t, sub), lambda: None)()
    term(z, 0)
    for sub in range(2):
        first, count = SUBS[sub]
        value = cbuf[0, first : first + count]
        for way in range(2):
            rs_copy(7, way, sub).wait_recv()
            value = value + rrecv[way, 7, first : first + count].astype(F32)
        dw_ref[first : first + count] = value

    for s in range(8):
        for sub in range(2):
            for way in range(2):
                if s < 7 or way == sub:
                    ag_copy(s, way, sub).wait_send()
                if s > 0 or way == sub:
                    rs_copy(s, way, sub).wait_send()

    @pl.loop(1, E)
    def _(k):
        peer = lax.rem(me + k, E)
        t_copy(peer, peer // SHARE, me, me).wait_send()
        p_copy(peer, peer, me, me).wait_send()


def on_device(tokens, expert_ids, slot_pos, smooth, smoothed_weight, act_grad):
    w = jnp.transpose(smoothed_weight, (1, 0, 2))
    w = jnp.pad(w, ((0, 0), (0, KP - KC), (0, HP - HID))).reshape(CH, HP)
    vmem = pl.BlockSpec(memory_space=pltpu.VMEM)
    dw, dtok = pl.pallas_call(
        kernel,
        out_shape=(
            jax.ShapeDtypeStruct((CH, HP), F32),
            jax.ShapeDtypeStruct((D, 128), BF16),
        ),
        in_specs=[vmem] * 6,
        out_specs=(vmem, vmem),
        scratch_shapes=[
            pltpu.VMEM((Z, CH, HP), BF16),
            pltpu.VMEM((4, BLK, WIDE), BF16),
            pltpu.VMEM((E, BLK, WIDE), BF16),
            pltpu.VMEM((4 * BLK, WIDE), F32),
            pltpu.VMEM((D + 64, ROWS), F32),
            pltpu.VMEM((Z, KP, ROWS), BF16),
            pltpu.VMEM((D + 64, 8), F32),
            pltpu.VMEM((2, ROWS, HP), F32),
            pltpu.VMEM((2, ROWS, HP), BF16),
            pltpu.VMEM((2, CH, HP), F32),
            pltpu.VMEM((2, 8, CH, HP), BF16),
            pltpu.VMEM((2, 8, CH, HP), BF16),
            pltpu.VMEM((3 * WIDE, ROWS), BF16),
            pltpu.VMEM((E, BLK, WIDE), BF16),
            pltpu.VMEM((E, BLK, WIDE), BF16),
            pltpu.SemaphoreType.DMA((2, 8, 2)),
            pltpu.SemaphoreType.DMA((2, 8, 2)),
            pltpu.SemaphoreType.DMA((2, 8, 2)),
            pltpu.SemaphoreType.DMA((2, 8, 2)),
            pltpu.SemaphoreType.DMA((E,)),
            pltpu.SemaphoreType.DMA((E,)),
            pltpu.SemaphoreType.DMA((E,)),
            pltpu.SemaphoreType.DMA((E,)),
        ],
        compiler_params=pltpu.CompilerParams(
            collective_id=0, has_side_effects=True, vmem_limit_bytes=48 * 1024 * 1024
        ),
    )(w, tokens[0].T, expert_ids[0].T, slot_pos[0].T, smooth, act_grad[0])
    dw = dw.reshape(2, KP, HP)[:, :KC, :HID].transpose(1, 0, 2)
    return dtok.T[None], dw


def solution(mesh):
    return jax.shard_map(
        on_device,
        mesh=mesh,
        in_specs=(
            P("dp", "ep", None),
            P("dp", "ep", None),
            P("dp", "ep", None),
            P(),
            P("dp", None, "ep"),
            P("dp", None, "ep"),
        ),
        out_specs=(P("dp", "ep", None), P("dp", None, "ep")),
        check_vma=False,
    )
```

```python
import functools

import jax
import jax.numpy as jnp
from jax import lax
from jax.experimental import pallas as pl
from jax.experimental.pallas import tpu as pltpu
from jax.sharding import PartitionSpec as P

MESH = pl.DeviceIdType.MESH
F32 = jnp.float32
BF16 = jnp.bfloat16
ALPHA = 1.702
Z = 16
E = 32
SHARE = 8
SLOT = 5
ROWS = 160
D = 2880
KC = 180
KP = 184
CH = 1040
HID = 360
HP = 384
WIDE = 1024
BLK = 16
THIRDS = ((0, 1024), (1024, 1024), (2048, 832))
C4, C5 = 736, 920
SUBS = ((0, 368), (368, 368), (736, 144), (880, 160))
N = len(SUBS)
FAR = (0, 2)


def mm(a, b):
    return jnp.dot(a, b, preferred_element_type=F32)


def mm_nt(a, b):
    return lax.dot_general(a, b, (((1,), (1,)), ((), ())), preferred_element_type=F32)


def mm_tn(a, b):
    return lax.dot_general(a, b, (((0,), (0,)), ((), ())), preferred_element_type=F32)


def kernel(
    w_ref, tok_ref, ids_ref, pos_ref, smooth_ref, act_ref,
    dw_ref, dtok_ref,
    wbuf, tsend, trecv, rows32, d32, sct, scy, scz, fcol, acc, gall, cbuf, rsend, rrecv, bthird, psend, precv, actc,
    ag_ss, ag_rs, rs_ss, rs_rs, t_ss, t_rs, p_ss, p_rs,
):
    z = lax.axis_index("dp")
    me = lax.axis_index("ep")
    right, left = lax.rem(z + 1, Z), lax.rem(z + Z - 1, Z)
    group = me // SHARE
    sides = (right, left)

    barrier = pltpu.get_barrier_semaphore()
    for side in sides:
        pl.semaphore_signal(barrier, inc=1, device_id={"dp": side}, device_id_type=MESH)

    @pl.loop(1, E)
    def _(k):
        pl.semaphore_signal(
            barrier, inc=1, device_id={"ep": lax.rem(me + k, E)}, device_id_type=MESH
        )

    def lanes(rows, low, high):
        lane = lax.broadcasted_iota(jnp.int32, (rows, 128), 1)
        return (lane >= low) & (lane < high)

    def roll(x, shift):
        return pltpu.roll(x, shift, 1)

    def own_chunk():
        for u in range(2):
            for half in range(2):
                at = half * 2 * KP + u * KP
                cbuf[0, at : at + KP] = w_ref[u, :, half * 128 : half * 128 + 128].astype(F32)
        gate = w_ref[0, :, 256:384].astype(F32)
        up = w_ref[1, :, 256:384].astype(F32)
        cbuf[0, C4:C5] = jnp.where(lanes(KP, 0, 104), gate, roll(up, 104))
        cbuf[0, C5:CH] = jnp.where(lanes(120, 0, 80), roll(up[0:120], 104), 0.0)
        low = up[120:180]
        cbuf[0, C5 : C5 + 60] = cbuf[0, C5 : C5 + 60] + jnp.where(
            lanes(60, 80, 128), roll(low, 56), 0.0
        )
        cbuf[0, C5 + 60 : CH] = cbuf[0, C5 + 60 : CH] + jnp.where(
            lanes(60, 80, 112), roll(low, 8), 0.0
        )
        wbuf[z] = cbuf[0].astype(BF16)

    own_chunk()
    pl.semaphore_wait(barrier, E + 1)

    def far(way, sub):
        return (sub in FAR) == (way == 0)

    def ag_copy(s, way, sub, owner):
        first, count = SUBS[sub]
        part = wbuf.at[owner, pl.ds(first, count)]
        return pltpu.make_async_remote_copy(
            src_ref=part, dst_ref=part,
            send_sem=ag_ss.at[way, s, sub], recv_sem=ag_rs.at[way, s, sub],
            device_id={"dp": sides[way]}, device_id_type=MESH,
        )

    def ag_send(s, way, sub):
        owner = lax.rem(z + Z - s, Z) if way == 0 else lax.rem(z + s, Z)
        return ag_copy(s, way, sub, owner)

    def ag_recv(s, way, sub):
        owner = lax.rem(z + Z - 1 - s, Z) if way == 0 else lax.rem(z + 1 + s, Z)
        return ag_copy(s, way, sub, owner)

    for sub in range(N):
        for way in range(2):
            ag_send(0, way, sub).start()

    def match_rows(count, shift):
        row = lax.broadcasted_iota(jnp.int32, (count, 128), 0)
        g = row >> shift
        j = row & (BLK - 1)
        slot = (j * 11) >> 5
        third = j - 3 * slot
        hit = jnp.zeros((count, 128), jnp.bool_)
        for k in range(4):
            hit = hit | ((ids_ref[k : k + 1, :] == g) & (pos_ref[k : k + 1, :] == slot))
        return [
            jnp.where(hit & (third == t), 1.0, 0.0).astype(BF16) for t in range(3)
        ]

    sel = match_rows(4 * BLK, 4)
    for t, (first, count) in enumerate(THIRDS):
        rows = mm_nt(sel[t], tok_ref[first : first + count, :])
        if t == 0:
            rows32[...] = rows
        else:
            rows32[:, 0:count] = rows32[:, 0:count] + rows
    for g in range(4):
        tsend[g] = rows32[g * BLK : (g + 1) * BLK, :].astype(BF16)

    def t_copy(peer, block, slot_at, peer_sem):
        return pltpu.make_async_remote_copy(
            src_ref=tsend.at[block], dst_ref=trecv.at[slot_at],
            send_sem=t_ss.at[peer], recv_sem=t_rs.at[peer_sem],
            device_id={"ep": peer}, device_id_type=MESH,
        )

    @pl.loop(1, E)
    def _(k):
        peer = lax.rem(me + k, E)
        t_copy(peer, peer // SHARE, me, me).start()

    trecv[me] = tsend[group]

    def place_rows(t, tall):
        shape = (E * BLK, ROWS) if tall else (ROWS, E * BLK)
        wide = lax.broadcasted_iota(jnp.int32, shape, 0 if tall else 1)
        r = lax.broadcasted_iota(jnp.int32, shape, 1 if tall else 0)
        s = (r * 205) >> 10
        return jnp.where(wide == s * BLK + (r - SLOT * s) * 3 + t, 1.0, 0.0).astype(BF16)

    def t_wait():
        @pl.loop(1, E)
        def _(k):
            peer = lax.rem(me + E - k, E)
            t_copy(peer, 0, peer, peer).wait_recv()

    def factors():
        row = smooth_ref[pl.ds(group, 1), :]
        for first, count in THIRDS:
            piece = jnp.broadcast_to(row[:, first : first + count], (8, count))
            fcol[first : first + count, :] = piece.T
        acc[...] = jnp.zeros_like(acc)
        actc[...] = jnp.zeros_like(actc)
        actc[:, 0:104] = act_ref[:, 256:360].astype(F32)

    def dispatch(t):
        first, count = THIRDS[t]
        wide = trecv[...].reshape(E * BLK, WIDE)
        rows = mm(place_rows(t, False), wide[:, 0:count])
        factor = smooth_ref[pl.ds(group, 1), first : first + count]
        scaled = (rows / factor).astype(BF16).astype(F32)
        d32[first : first + count, :] = scaled.T
        if t == 2:
            d32[D : D + 64, :] = jnp.zeros((64, ROWS), F32)

    def chunks(low, high):
        for o in range(low, high):
            at = KC * o
            row = lax.broadcasted_iota(jnp.int32, (KP, ROWS), 0)
            sct[o] = jnp.where(row < KC, d32[at : at + KP, :], 0.0).astype(BF16)
            row = lax.broadcasted_iota(jnp.int32, (120, ROWS), 0)
            scy[o] = jnp.where(row < 60, d32[at + 120 : at + 240, :], 0.0).astype(BF16)
            scz[o] = jnp.where(row >= 60, d32[at + 60 : at + 180, :], 0.0).astype(BF16)

    def forward(o, part):
        if part < 2:
            first = 2 * KP * part
            pair = jnp.concatenate(
                [wbuf[o, first : first + KP], wbuf[o, first + KP : first + 2 * KP]], axis=1
            )
            at = 256 * part
            acc[:, at : at + 256] = acc[:, at : at + 256] + mm_tn(sct[o], pair)
        else:
            block = wbuf[o, C5:CH]
            acc[:, 512:640] = acc[:, 512:640] + mm_tn(sct[o], wbuf[o, C4:C5])
            acc[:, 640:768] = acc[:, 640:768] + mm_tn(sct[o, 0:120], block)
            acc[:, 768:896] = acc[:, 768:896] + mm_tn(scy[o], block)
            acc[:, 896:1024] = acc[:, 896:1024] + mm_tn(scz[o], block)

    def forward_at(*steps):
        for d in steps:
            for part in range(3):
                forward(lax.rem(z + Z + d, Z), part)

    def forward_pair(d, part):
        forward(lax.rem(z + Z + d, Z), part)
        forward(lax.rem(z + Z - d, Z), part)

    ag_tasks = {
        (1, 0): factors,
        (3, 0): lambda: (t_wait(), dispatch(0)),
        (3, 1): lambda: dispatch(1),
        (3, 2): lambda: dispatch(2),
        (3, 3): lambda: chunks(0, 4),
        (4, 0): lambda: chunks(4, 8),
        (4, 1): lambda: chunks(8, 12),
        (4, 2): lambda: chunks(12, 16),
        (4, 3): lambda: forward_at(0, 1),
        (5, 0): lambda: forward_at(-1, 2),
        (5, 1): lambda: forward_at(-2, 3),
        (5, 2): lambda: forward_at(-3, 4),
        (5, 3): lambda: forward_at(-4, 5),
        (6, 0): lambda: forward_at(-5),
        (6, 3): lambda: forward_at(-6, 6),
        (7, 0): lambda: forward_pair(7, 0),
        (7, 1): lambda: forward_pair(7, 1),
        (7, 3): lambda: forward_pair(7, 2),
    }
    for s in range(1, 8):
        for sub in range(N):
            for way in range(2):
                ag_recv(s - 1, way, sub).wait_recv()
                if s < 7 or far(way, sub):
                    ag_send(s, way, sub).start()
            ag_tasks.get((s, sub), lambda: None)()

    def gradients(gate, up, c):
        q = 1.0 / (1.0 + jnp.exp(-ALPHA * gate))
        gg = c * (up + 1.0) * q * (1.0 + ALPHA * gate * (1.0 - q))
        return gg, c * gate * q

    def activate(part):
        at = 256 * part
        if part < 2:
            c = act_ref[:, 128 * part : 128 * part + 128].astype(F32)
            gg, gu = gradients(acc[:, at : at + 128], acc[:, at + 128 : at + 256], c)
            gall[:, at : at + 128] = gg.astype(BF16)
            gall[:, at + 128 : at + 256] = gu.astype(BF16)
            return
        gate = acc[:, 512:640]
        up = jnp.where(lanes(ROWS, 0, 24), roll(gate, 24), 0.0)
        up = jnp.where(lanes(ROWS, 24, 104), roll(acc[:, 640:768], 24), up)
        up = up + jnp.where(lanes(ROWS, 24, 72), roll(acc[:, 768:896], 72), 0.0)
        up = up + jnp.where(lanes(ROWS, 72, 104), roll(acc[:, 896:1024], 120), 0.0)
        gg, gu = gradients(gate, up, actc[...])
        turned = roll(gu, 104)
        gall[:, 512:640] = jnp.where(lanes(ROWS, 0, 104), gg, turned).astype(BF16)
        gall[:, 640:768] = jnp.where(lanes(ROWS, 0, 80), turned, 0.0).astype(BF16)
        gall[:, 768:896] = jnp.where(lanes(ROWS, 80, 128), roll(gu, 56), 0.0).astype(BF16)
        gall[:, 896:1024] = jnp.where(lanes(ROWS, 80, 112), roll(gu, 8), 0.0).astype(BF16)

    def term(o, part, at):
        if part < 2:
            pair = mm(sct[o], gall[:, 256 * part : 256 * part + 256])
            first = 2 * KP * part
            cbuf[at, first : first + KP] = pair[:, 0:128]
            cbuf[at, first + KP : first + 2 * KP] = pair[:, 128:256]
        else:
            cbuf[at, C4:C5] = mm(sct[o], gall[:, 512:640])
            cbuf[at, C5:CH] = (
                mm(sct[o, 0:120], gall[:, 640:768])
                + mm(scy[o], gall[:, 768:896])
                + mm(scz[o], gall[:, 896:1024])
            )

    def rs_copy(t, way, sub):
        first, count = SUBS[sub]
        return pltpu.make_async_remote_copy(
            src_ref=rsend.at[way, t, pl.ds(first, count)],
            dst_ref=rrecv.at[way, t, pl.ds(first, count)],
            send_sem=rs_ss.at[way, t, sub], recv_sem=rs_rs.at[way, t, sub],
            device_id={"dp": sides[way]}, device_id_type=MESH,
        )

    def rs_send(t, way, sub, at, add):
        first, count = SUBS[sub]
        value = cbuf[at, first : first + count]
        if add:
            rs_copy(t - 1, way, sub).wait_recv()
            value = value + rrecv[way, t - 1, first : first + count].astype(F32)
        rsend[way, t, first : first + count] = value.astype(BF16)
        rs_copy(t, way, sub).start()

    def owner(t, way):
        return lax.rem(z + 8 - t + Z, Z) if way == 0 else lax.rem(z + 8 + t, Z)

    def turn(part, subs):
        opposite = lax.rem(z + 8, Z)
        for sub in subs:
            ag_recv(7, 0 if far(0, sub) else 1, sub).wait_recv()
        forward(opposite, part)
        activate(part)
        term(opposite, part, 0)
        for sub in subs:
            rs_send(0, 0 if far(0, sub) else 1, sub, 0, False)
        for way in range(2):
            if any(not far(way, sub) for sub in subs):
                term(owner(1, way), part, 1)
                for sub in subs:
                    if not far(way, sub):
                        rs_send(1, way, sub, 1, False)

    turn(0, (0,))
    turn(1, (1,))
    turn(2, (2, 3))

    def back(low, high):
        for o in range(low, high):
            pairs = jnp.concatenate(
                [wbuf[o, first : first + KP] for first in range(0, C5, KP)], axis=1
            )
            block = wbuf[o, C5:CH]
            at = KC * o
            d32[at : at + KP, :] = mm_nt(pairs, gall[:, 0:640])
            d32[at : at + 120, :] = d32[at : at + 120, :] + mm_nt(block, gall[:, 640:768])
            low_rows = mm_nt(block, gall[:, 768:896])
            high_rows = mm_nt(block, gall[:, 896:1024])
            d32[at + 120 : at + 180, :] = (
                d32[at + 120 : at + 180, :] + low_rows[0:60] + high_rows[60:120]
            )

    def unscale():
        for first, count in THIRDS:
            bthird[first : first + count, :] = (
                d32[first : first + count, :] / fcol[first : first + count, 0:1]
            ).astype(BF16)
        bthird[D : 3 * WIDE, :] = jnp.zeros((3 * WIDE - D, ROWS), BF16)

    def expand():
        total = None
        for t in range(3):
            rows = mm_nt(place_rows(t, True), bthird[WIDE * t : WIDE * (t + 1), :])
            total = rows if total is None else total + rows
        psend[...] = total.astype(BF16).reshape(E, BLK, WIDE)

    def p_copy(peer, block, slot_at, peer_sem):
        return pltpu.make_async_remote_copy(
            src_ref=psend.at[block], dst_ref=precv.at[slot_at],
            send_sem=p_ss.at[peer], recv_sem=p_rs.at[peer_sem],
            device_id={"ep": peer}, device_id_type=MESH,
        )

    def p_start():
        @pl.loop(1, E)
        def _(k):
            peer = lax.rem(me + k, E)
            p_copy(peer, peer, me, me).start()

        precv[me] = psend[me]

    def p_wait():
        @pl.loop(1, E)
        def _(k):
            peer = lax.rem(me + E - k, E)
            p_copy(peer, 0, peer, peer).wait_recv()

    def combine(t, pick):
        first, count = THIRDS[t]
        flat = precv[...].reshape(E * BLK, WIDE)
        dtok_ref[first : first + count, :] = mm_tn(flat[:, 0:count], pick[t]).astype(BF16)

    def combine_all():
        pick = match_rows(E * BLK, 7)
        for t in range(3):
            combine(t, pick)

    rs_tasks = {
        (1, 0): lambda: back(0, 4),
        (1, 1): lambda: back(4, 8),
        (1, 3): lambda: back(8, 12),
        (2, 0): lambda: back(12, 16),
        (2, 1): unscale,
        (2, 3): lambda: (expand(), p_start()),
        (6, 0): lambda: (p_wait(), combine_all()),
    }
    for t in range(1, 8):
        for sub in range(N):
            for way in range(2):
                if t == 1 and not far(way, sub):
                    continue
                if sub < 3:
                    term(owner(t, way), sub, way)
                elif t == 1:
                    term(owner(t, way), 2, way)
                rs_send(t, way, sub, way, True)
            rs_tasks.get((t, sub), lambda: None)()
    for sub in range(N):
        first, count = SUBS[sub]
        if sub < 3:
            term(z, sub, 0)
        value = cbuf[0, first : first + count]
        for way in range(2):
            rs_copy(7, way, sub).wait_recv()
            value = value + rrecv[way, 7, first : first + count].astype(F32)
        cbuf[1, first : first + count] = value
        if sub < 2:
            dw_ref[0, :, 128 * sub : 128 * sub + 128] = value[0:KP]
            dw_ref[1, :, 128 * sub : 128 * sub + 128] = value[KP : 2 * KP]
    mixed = cbuf[1, C4:C5]
    dw_ref[0, :, 256:384] = mixed
    dw_ref[1, :, 256:384] = jnp.where(lanes(KP, 0, 24), roll(mixed, 24), 0.0)
    dw_ref[1, 0:120, 256:384] = jnp.where(
        lanes(120, 24, 104), roll(cbuf[1, C5:CH], 24), dw_ref[1, 0:120, 256:384]
    )
    low = jnp.where(lanes(60, 24, 72), roll(cbuf[1, C5 : C5 + 60], 72), 0.0)
    high = jnp.where(lanes(60, 72, 104), roll(cbuf[1, C5 + 60 : CH], 120), 0.0)
    dw_ref[1, 120:180, 256:384] = dw_ref[1, 120:180, 256:384] + low + high

    for s in range(8):
        for sub in range(N):
            for way in range(2):
                if s < 7 or far(way, sub):
                    ag_send(s, way, sub).wait_send()
                if s > 0 or far(way, sub):
                    rs_copy(s, way, sub).wait_send()

    @pl.loop(1, E)
    def _(k):
        peer = lax.rem(me + k, E)
        t_copy(peer, peer // SHARE, me, me).wait_send()
        p_copy(peer, peer, me, me).wait_send()


def on_device(tokens, expert_ids, slot_pos, smooth, smoothed_weight, act_grad):
    w = jnp.transpose(smoothed_weight, (1, 0, 2))
    w = jnp.pad(w, ((0, 0), (0, KP - KC), (0, HP - HID)))
    vmem = pl.BlockSpec(memory_space=pltpu.VMEM)
    dw, dtok = pl.pallas_call(
        kernel,
        out_shape=(
            jax.ShapeDtypeStruct((2, KP, HP), F32),
            jax.ShapeDtypeStruct((D, 128), BF16),
        ),
        in_specs=[vmem] * 6,
        out_specs=(vmem, vmem),
        scratch_shapes=[
            pltpu.VMEM((Z, CH, 128), BF16),
            pltpu.VMEM((4, BLK, WIDE), BF16),
            pltpu.VMEM((E, BLK, WIDE), BF16),
            pltpu.VMEM((4 * BLK, WIDE), F32),
            pltpu.VMEM((D + 64, ROWS), F32),
            pltpu.VMEM((Z, KP, ROWS), BF16),
            pltpu.VMEM((Z, 120, ROWS), BF16),
            pltpu.VMEM((Z, 120, ROWS), BF16),
            pltpu.VMEM((D, 8), F32),
            pltpu.VMEM((ROWS, 1024), F32),
            pltpu.VMEM((ROWS, 1024), BF16),
            pltpu.VMEM((2, CH, 128), F32),
            pltpu.VMEM((2, 8, CH, 128), BF16),
            pltpu.VMEM((2, 8, CH, 128), BF16),
            pltpu.VMEM((3 * WIDE, ROWS), BF16),
            pltpu.VMEM((E, BLK, WIDE), BF16),
            pltpu.VMEM((E, BLK, WIDE), BF16),
            pltpu.VMEM((ROWS, 128), F32),
            pltpu.SemaphoreType.DMA((2, 8, N)),
            pltpu.SemaphoreType.DMA((2, 8, N)),
            pltpu.SemaphoreType.DMA((2, 8, N)),
            pltpu.SemaphoreType.DMA((2, 8, N)),
            pltpu.SemaphoreType.DMA((E,)),
            pltpu.SemaphoreType.DMA((E,)),
            pltpu.SemaphoreType.DMA((E,)),
            pltpu.SemaphoreType.DMA((E,)),
        ],
        compiler_params=pltpu.CompilerParams(
            collective_id=0, has_side_effects=True, vmem_limit_bytes=48 * 1024 * 1024
        ),
    )(w, tokens[0].T, expert_ids[0].T, slot_pos[0].T, smooth, act_grad[0])
    dw = dw[:, :KC, :HID].transpose(1, 0, 2)
    return dtok.T[None], dw


def solution(mesh):
    return jax.shard_map(
        on_device,
        mesh=mesh,
        in_specs=(
            P("dp", "ep", None),
            P("dp", "ep", None),
            P("dp", "ep", None),
            P(),
            P("dp", None, "ep"),
            P("dp", None, "ep"),
        ),
        out_specs=(P("dp", "ep", None), P("dp", None, "ep")),
        check_vma=False,
    )
```

```python
import functools

import jax
import jax.numpy as jnp
from jax import lax
from jax.experimental import pallas as pl
from jax.experimental.pallas import tpu as pltpu
from jax.sharding import PartitionSpec as P

MESH = pl.DeviceIdType.MESH
F32 = jnp.float32
BF16 = jnp.bfloat16
ALPHA = 1.702
Z = 16
E = 32
SHARE = 8
SLOT = 5
ROWS = 160
D = 2880
KC = 180
KP = 184
CH = 1040
HID = 360
HP = 384
WIDE = 1024
BLK = 16
THIRDS = ((0, 1024), (1024, 1024), (2048, 832))
C4, C5 = 736, 920
SUBS = ((0, 368), (368, 368), (736, 144), (880, 160))
N = len(SUBS)
FAR = (0, 2)


def mm(a, b):
    return jnp.dot(a, b, preferred_element_type=F32)


def mm_nt(a, b):
    return lax.dot_general(a, b, (((1,), (1,)), ((), ())), preferred_element_type=F32)


def mm_tn(a, b):
    return lax.dot_general(a, b, (((0,), (0,)), ((), ())), preferred_element_type=F32)


def kernel(
    w_ref, tok_ref, ids_ref, pos_ref, smooth_ref, act_ref,
    dw_ref, dtok_ref,
    tok_vm, tok_sem, wbuf, tsend, trecv, rows32, d32, sct, scy, scz, fcol, acc, gall, cbuf, rsend, rrecv, bthird, psend, precv, actc,
    ag_ss, ag_rs, rs_ss, rs_rs, t_ss, t_rs, p_ss, p_rs,
):
    z = lax.axis_index("dp")
    me = lax.axis_index("ep")
    right, left = lax.rem(z + 1, Z), lax.rem(z + Z - 1, Z)
    group = me // SHARE
    sides = (right, left)

    barrier = pltpu.get_barrier_semaphore()
    for side in sides:
        pl.semaphore_signal(barrier, inc=1, device_id={"dp": side}, device_id_type=MESH)

    @pl.loop(1, E)
    def _(k):
        pl.semaphore_signal(
            barrier, inc=1, device_id={"ep": lax.rem(me + k, E)}, device_id_type=MESH
        )

    tok_load = pltpu.make_async_copy(tok_ref, tok_vm, tok_sem)
    tok_load.start()

    def lanes(rows, low, high):
        lane = lax.broadcasted_iota(jnp.int32, (rows, 128), 1)
        return (lane >= low) & (lane < high)

    def roll(x, shift):
        return pltpu.roll(x, shift, 1)

    def own_chunk():
        for u in range(2):
            for half in range(2):
                at = half * 2 * KP + u * KP
                cbuf[0, at : at + KP] = w_ref[u, :, half * 128 : half * 128 + 128].astype(F32)
        gate = w_ref[0, :, 256:384].astype(F32)
        up = w_ref[1, :, 256:384].astype(F32)
        cbuf[0, C4:C5] = jnp.where(lanes(KP, 0, 104), gate, roll(up, 104))
        cbuf[0, C5:CH] = jnp.where(lanes(120, 0, 80), roll(up[0:120], 104), 0.0)
        low = up[120:180]
        cbuf[0, C5 : C5 + 60] = cbuf[0, C5 : C5 + 60] + jnp.where(
            lanes(60, 80, 128), roll(low, 56), 0.0
        )
        cbuf[0, C5 + 60 : CH] = cbuf[0, C5 + 60 : CH] + jnp.where(
            lanes(60, 80, 112), roll(low, 8), 0.0
        )
        wbuf[z] = cbuf[0].astype(BF16)

    own_chunk()
    pl.semaphore_wait(barrier, E + 1)

    def far(way, sub):
        return (sub in FAR) == (way == 0)

    def ag_copy(s, way, sub, owner):
        first, count = SUBS[sub]
        part = wbuf.at[owner, pl.ds(first, count)]
        return pltpu.make_async_remote_copy(
            src_ref=part, dst_ref=part,
            send_sem=ag_ss.at[way, s, sub], recv_sem=ag_rs.at[way, s, sub],
            device_id={"dp": sides[way]}, device_id_type=MESH,
        )

    def ag_send(s, way, sub):
        owner = lax.rem(z + Z - s, Z) if way == 0 else lax.rem(z + s, Z)
        return ag_copy(s, way, sub, owner)

    def ag_recv(s, way, sub):
        owner = lax.rem(z + Z - 1 - s, Z) if way == 0 else lax.rem(z + 1 + s, Z)
        return ag_copy(s, way, sub, owner)

    def ag_sent(s):
        for sub in range(N):
            for way in range(2):
                if s < 7 or far(way, sub):
                    ag_send(s, way, sub).wait_send()

    for sub in range(N):
        for way in range(2):
            ag_send(0, way, sub).start()

    def match_rows(count, shift):
        row = lax.broadcasted_iota(jnp.int32, (count, 128), 0)
        g = row >> shift
        j = row & (BLK - 1)
        slot = (j * 11) >> 5
        third = j - 3 * slot
        hit = jnp.zeros((count, 128), jnp.bool_)
        for k in range(4):
            hit = hit | ((ids_ref[k : k + 1, :] == g) & (pos_ref[k : k + 1, :] == slot))
        return [
            jnp.where(hit & (third == t), 1.0, 0.0).astype(BF16) for t in range(3)
        ]

    tok_load.wait()
    sel = match_rows(4 * BLK, 4)
    for t, (first, count) in enumerate(THIRDS):
        rows = mm_nt(sel[t], tok_vm[first : first + count, :])
        if t == 0:
            rows32[...] = rows
        else:
            rows32[:, 0:count] = rows32[:, 0:count] + rows
    for g in range(4):
        tsend[g] = rows32[g * BLK : (g + 1) * BLK, :].astype(BF16)

    def t_copy(peer, block, slot_at, peer_sem):
        return pltpu.make_async_remote_copy(
            src_ref=tsend.at[block], dst_ref=trecv.at[slot_at],
            send_sem=t_ss.at[peer], recv_sem=t_rs.at[peer_sem],
            device_id={"ep": peer}, device_id_type=MESH,
        )

    @pl.loop(1, E)
    def _(k):
        peer = lax.rem(me + k, E)
        t_copy(peer, peer // SHARE, me, me).start()

    trecv[me] = tsend[group]

    def place_rows(t, tall, first=0, count=E * BLK):
        shape = (count, ROWS) if tall else (ROWS, count)
        wide = lax.broadcasted_iota(jnp.int32, shape, 0 if tall else 1) + first
        r = lax.broadcasted_iota(jnp.int32, shape, 1 if tall else 0)
        s = (r * 205) >> 10
        return jnp.where(wide == s * BLK + (r - SLOT * s) * 3 + t, 1.0, 0.0).astype(BF16)

    def t_sent():
        @pl.loop(1, E)
        def _(k):
            peer = lax.rem(me + k, E)
            t_copy(peer, peer // SHARE, me, me).wait_send()

    def t_wait():
        @pl.loop(1, E)
        def _(k):
            peer = lax.rem(me + E - k, E)
            t_copy(peer, 0, peer, peer).wait_recv()

    def factors():
        row = smooth_ref[pl.ds(group, 1), :]
        for first, count in THIRDS:
            piece = jnp.broadcast_to(row[:, first : first + count], (8, count))
            fcol[first : first + count, :] = piece.T
        acc[...] = jnp.zeros_like(acc)
        actc[...] = jnp.zeros_like(actc)
        actc[:, 0:104] = act_ref[:, 256:360].astype(F32)

    def dispatch(t):
        first, count = THIRDS[t]
        wide = trecv[...].reshape(E * BLK, WIDE)
        rows = mm(place_rows(t, False), wide[:, 0:count])
        factor = smooth_ref[pl.ds(group, 1), first : first + count]
        scaled = (rows / factor).astype(BF16).astype(F32)
        d32[first : first + count, :] = scaled.T
        if t == 2:
            d32[D : D + 64, :] = jnp.zeros((64, ROWS), F32)

    def chunks(low, high):
        for o in range(low, high):
            at = KC * o
            row = lax.broadcasted_iota(jnp.int32, (KP, ROWS), 0)
            sct[o] = jnp.where(row < KC, d32[at : at + KP, :], 0.0).astype(BF16)
            row = lax.broadcasted_iota(jnp.int32, (120, ROWS), 0)
            scy[o] = jnp.where(row < 60, d32[at + 120 : at + 240, :], 0.0).astype(BF16)
            scz[o] = jnp.where(row >= 60, d32[at + 60 : at + 180, :], 0.0).astype(BF16)

    def forward(o, part):
        if part < 2:
            first = 2 * KP * part
            pair = jnp.concatenate(
                [wbuf[o, first : first + KP], wbuf[o, first + KP : first + 2 * KP]], axis=1
            )
            at = 256 * part
            acc[:, at : at + 256] = acc[:, at : at + 256] + mm_tn(sct[o], pair)
        else:
            block = wbuf[o, C5:CH]
            acc[:, 512:640] = acc[:, 512:640] + mm_tn(sct[o], wbuf[o, C4:C5])
            acc[:, 640:768] = acc[:, 640:768] + mm_tn(sct[o, 0:120], block)
            acc[:, 768:896] = acc[:, 768:896] + mm_tn(scy[o], block)
            acc[:, 896:1024] = acc[:, 896:1024] + mm_tn(scz[o], block)

    def forward_at(*steps):
        for d in steps:
            for part in range(3):
                forward(lax.rem(z + Z + d, Z), part)

    def forward_pair(d, part):
        forward(lax.rem(z + Z + d, Z), part)
        forward(lax.rem(z + Z - d, Z), part)

    ag_tasks = {
        (1, 0): factors,
        (3, 1): lambda: (t_wait(), dispatch(0)),
        (3, 2): lambda: dispatch(1),
        (3, 3): lambda: dispatch(2),
        (4, 0): lambda: chunks(0, 4),
        (4, 1): lambda: chunks(4, 8),
        (4, 2): lambda: chunks(8, 12),
        (4, 3): lambda: chunks(12, 16),
        (5, 0): lambda: forward_at(0, 1),
        (5, 1): lambda: forward_at(-1, 2),
        (5, 2): lambda: forward_at(-2, 3),
        (5, 3): lambda: forward_at(-3, 4),
        (6, 0): lambda: forward_at(-4, 5),
        (6, 1): lambda: forward_at(-5),
        (6, 2): t_sent,
        (6, 3): lambda: forward_at(-6),
        (7, 0): lambda: (forward_pair(7, 0), forward(lax.rem(z + 6, Z), 0)),
        (7, 1): lambda: (forward_pair(7, 1), forward(lax.rem(z + 6, Z), 1)),
        (7, 2): lambda: forward(lax.rem(z + 6, Z), 2),
        (7, 3): lambda: forward_pair(7, 2),
    }
    for s in range(1, 8):
        for sub in range(N):
            for way in range(2):
                ag_recv(s - 1, way, sub).wait_recv()
                if s < 7 or far(way, sub):
                    ag_send(s, way, sub).start()
            ag_tasks.get((s, sub), lambda: None)()
        if s > 1:
            ag_sent(s - 2)

    def gradients(gate, up, c):
        q = 1.0 / (1.0 + jnp.exp(-ALPHA * gate))
        gg = c * (up + 1.0) * q * (1.0 + ALPHA * gate * (1.0 - q))
        return gg, c * gate * q

    def activate(part):
        at = 256 * part
        if part < 2:
            c = act_ref[:, 128 * part : 128 * part + 128].astype(F32)
            gg, gu = gradients(acc[:, at : at + 128], acc[:, at + 128 : at + 256], c)
            gall[:, at : at + 128] = gg.astype(BF16)
            gall[:, at + 128 : at + 256] = gu.astype(BF16)
            return
        gate = acc[:, 512:640]
        up = jnp.where(lanes(ROWS, 0, 24), roll(gate, 24), 0.0)
        up = jnp.where(lanes(ROWS, 24, 104), roll(acc[:, 640:768], 24), up)
        up = up + jnp.where(lanes(ROWS, 24, 72), roll(acc[:, 768:896], 72), 0.0)
        up = up + jnp.where(lanes(ROWS, 72, 104), roll(acc[:, 896:1024], 120), 0.0)
        gg, gu = gradients(gate, up, actc[...])
        turned = roll(gu, 104)
        gall[:, 512:640] = jnp.where(lanes(ROWS, 0, 104), gg, turned).astype(BF16)
        gall[:, 640:768] = jnp.where(lanes(ROWS, 0, 80), turned, 0.0).astype(BF16)
        gall[:, 768:896] = jnp.where(lanes(ROWS, 80, 128), roll(gu, 56), 0.0).astype(BF16)
        gall[:, 896:1024] = jnp.where(lanes(ROWS, 80, 112), roll(gu, 8), 0.0).astype(BF16)

    def term(o, part, at):
        if part < 2:
            pair = mm(sct[o], gall[:, 256 * part : 256 * part + 256])
            first = 2 * KP * part
            cbuf[at, first : first + KP] = pair[:, 0:128]
            cbuf[at, first + KP : first + 2 * KP] = pair[:, 128:256]
        else:
            cbuf[at, C4:C5] = mm(sct[o], gall[:, 512:640])
            cbuf[at, C5:CH] = (
                mm(sct[o, 0:120], gall[:, 640:768])
                + mm(scy[o], gall[:, 768:896])
                + mm(scz[o], gall[:, 896:1024])
            )

    def rs_copy(t, way, sub):
        first, count = SUBS[sub]
        return pltpu.make_async_remote_copy(
            src_ref=rsend.at[way, t, pl.ds(first, count)],
            dst_ref=rrecv.at[way, t, pl.ds(first, count)],
            send_sem=rs_ss.at[way, t, sub], recv_sem=rs_rs.at[way, t, sub],
            device_id={"dp": sides[way]}, device_id_type=MESH,
        )

    def rs_send(t, way, sub, at, add):
        first, count = SUBS[sub]
        value = cbuf[at, first : first + count]
        if add:
            rs_copy(t - 1, way, sub).wait_recv()
            value = value + rrecv[way, t - 1, first : first + count].astype(F32)
        rsend[way, t, first : first + count] = value.astype(BF16)
        rs_copy(t, way, sub).start()

    def rs_sent(t):
        for sub in range(N):
            for way in range(2):
                if t > 0 or far(way, sub):
                    rs_copy(t, way, sub).wait_send()

    def owner(t, way):
        return lax.rem(z + 8 - t + Z, Z) if way == 0 else lax.rem(z + 8 + t, Z)

    def turn(part, subs):
        opposite = lax.rem(z + 8, Z)
        for sub in subs:
            ag_recv(7, 0 if far(0, sub) else 1, sub).wait_recv()
        forward(opposite, part)
        activate(part)
        term(opposite, part, 0)
        for sub in subs:
            rs_send(0, 0 if far(0, sub) else 1, sub, 0, False)
        for way in range(2):
            if any(not far(way, sub) for sub in subs):
                term(owner(1, way), part, 1)
                for sub in subs:
                    if not far(way, sub):
                        rs_send(1, way, sub, 1, False)

    turn(0, (0,))
    turn(1, (1,))
    turn(2, (2, 3))

    def back(low, high):
        for o in range(low, high):
            pairs = jnp.concatenate(
                [wbuf[o, first : first + KP] for first in range(0, C5, KP)], axis=1
            )
            block = wbuf[o, C5:CH]
            at = KC * o
            d32[at : at + KP, :] = mm_nt(pairs, gall[:, 0:640])
            d32[at : at + 120, :] = d32[at : at + 120, :] + mm_nt(block, gall[:, 640:768])
            low_rows = mm_nt(block, gall[:, 768:896])
            high_rows = mm_nt(block, gall[:, 896:1024])
            d32[at + 120 : at + 180, :] = (
                d32[at + 120 : at + 180, :] + low_rows[0:60] + high_rows[60:120]
            )

    def unscale():
        for first, count in THIRDS:
            bthird[first : first + count, :] = (
                d32[first : first + count, :] / fcol[first : first + count, 0:1]
            ).astype(BF16)
        bthird[D : 3 * WIDE, :] = jnp.zeros((3 * WIDE - D, ROWS), BF16)

    def expand(half):
        first = half * (E // 2) * BLK
        total = None
        for t in range(3):
            place = place_rows(t, True, first, (E // 2) * BLK)
            rows = mm_nt(place, bthird[WIDE * t : WIDE * (t + 1), :])
            total = rows if total is None else total + rows
        at = half * (E // 2)
        psend[at : at + E // 2] = total.astype(BF16).reshape(E // 2, BLK, WIDE)

    def p_copy(peer, block, slot_at, peer_sem):
        return pltpu.make_async_remote_copy(
            src_ref=psend.at[block], dst_ref=precv.at[slot_at],
            send_sem=p_ss.at[peer], recv_sem=p_rs.at[peer_sem],
            device_id={"ep": peer}, device_id_type=MESH,
        )

    def p_start():
        @pl.loop(1, E)
        def _(k):
            peer = lax.rem(me + k, E)
            p_copy(peer, peer, me, me).start()

        precv[me] = psend[me]

    def p_sent():
        @pl.loop(1, E)
        def _(k):
            peer = lax.rem(me + k, E)
            p_copy(peer, peer, me, me).wait_send()

    def p_wait():
        @pl.loop(1, E)
        def _(k):
            peer = lax.rem(me + E - k, E)
            p_copy(peer, 0, peer, peer).wait_recv()

    def combine(t):
        first, count = THIRDS[t]
        flat = precv[...].reshape(E * BLK, WIDE)
        pick = match_rows(E * BLK, 7)[t]
        dtok_ref[first : first + count, :] = mm_tn(flat[:, 0:count], pick).astype(BF16)

    rs_tasks = {
        (1, 0): lambda: back(0, 2),
        (1, 1): lambda: back(2, 4),
        (1, 2): lambda: back(4, 6),
        (1, 3): lambda: back(6, 8),
        (2, 0): lambda: back(8, 10),
        (2, 1): lambda: back(10, 12),
        (2, 2): lambda: back(12, 14),
        (2, 3): lambda: back(14, 16),
        (3, 0): unscale,
        (3, 1): lambda: expand(0),
        (3, 2): lambda: expand(1),
        (3, 3): p_start,
        (6, 1): lambda: (p_wait(), combine(0)),
        (6, 2): lambda: combine(1),
        (6, 3): lambda: combine(2),
        (7, 0): p_sent,
    }
    for t in range(1, 8):
        for sub in range(N):
            for way in range(2):
                if t == 1 and not far(way, sub):
                    continue
                if sub < 3:
                    term(owner(t, way), sub, way)
                elif t == 1:
                    term(owner(t, way), 2, way)
                rs_send(t, way, sub, way, True)
            rs_tasks.get((t, sub), lambda: None)()
        if t < 3:
            ag_sent(5 + t)
        else:
            rs_sent(t - 3)
    for sub in range(N):
        first, count = SUBS[sub]
        if sub < 3:
            term(z, sub, 0)
        value = cbuf[0, first : first + count]
        for way in range(2):
            rs_copy(7, way, sub).wait_recv()
            value = value + rrecv[way, 7, first : first + count].astype(F32)
        cbuf[1, first : first + count] = value
        if sub < 2:
            dw_ref[0, :, 128 * sub : 128 * sub + 128] = value[0:KP]
            dw_ref[1, :, 128 * sub : 128 * sub + 128] = value[KP : 2 * KP]
    mixed = cbuf[1, C4:C5]
    dw_ref[0, :, 256:384] = mixed
    dw_ref[1, :, 256:384] = jnp.where(lanes(KP, 0, 24), roll(mixed, 24), 0.0)
    dw_ref[1, 0:120, 256:384] = jnp.where(
        lanes(120, 24, 104), roll(cbuf[1, C5:CH], 24), dw_ref[1, 0:120, 256:384]
    )
    low = jnp.where(lanes(60, 24, 72), roll(cbuf[1, C5 : C5 + 60], 72), 0.0)
    high = jnp.where(lanes(60, 72, 104), roll(cbuf[1, C5 + 60 : CH], 120), 0.0)
    dw_ref[1, 120:180, 256:384] = dw_ref[1, 120:180, 256:384] + low + high

    for t in range(5, 8):
        rs_sent(t)


def on_device(tokens, expert_ids, slot_pos, smooth, smoothed_weight, act_grad):
    w = jnp.transpose(smoothed_weight, (1, 0, 2))
    w = jnp.pad(w, ((0, 0), (0, KP - KC), (0, HP - HID)))
    vmem = pl.BlockSpec(memory_space=pltpu.VMEM)
    dw, dtok = pl.pallas_call(
        kernel,
        out_shape=(
            jax.ShapeDtypeStruct((2, KP, HP), F32),
            jax.ShapeDtypeStruct((D, 128), BF16),
        ),
        in_specs=[vmem, pl.BlockSpec(memory_space=pl.ANY)] + [vmem] * 4,
        out_specs=(vmem, vmem),
        scratch_shapes=[
            pltpu.VMEM((D, 128), BF16),
            pltpu.SemaphoreType.DMA,
            pltpu.VMEM((Z, CH, 128), BF16),
            pltpu.VMEM((4, BLK, WIDE), BF16),
            pltpu.VMEM((E, BLK, WIDE), BF16),
            pltpu.VMEM((4 * BLK, WIDE), F32),
            pltpu.VMEM((D + 64, ROWS), F32),
            pltpu.VMEM((Z, KP, ROWS), BF16),
            pltpu.VMEM((Z, 120, ROWS), BF16),
            pltpu.VMEM((Z, 120, ROWS), BF16),
            pltpu.VMEM((D, 8), F32),
            pltpu.VMEM((ROWS, 1024), F32),
            pltpu.VMEM((ROWS, 1024), BF16),
            pltpu.VMEM((2, CH, 128), F32),
            pltpu.VMEM((2, 8, CH, 128), BF16),
            pltpu.VMEM((2, 8, CH, 128), BF16),
            pltpu.VMEM((3 * WIDE, ROWS), BF16),
            pltpu.VMEM((E, BLK, WIDE), BF16),
            pltpu.VMEM((E, BLK, WIDE), BF16),
            pltpu.VMEM((ROWS, 128), F32),
            pltpu.SemaphoreType.DMA((2, 8, N)),
            pltpu.SemaphoreType.DMA((2, 8, N)),
            pltpu.SemaphoreType.DMA((2, 8, N)),
            pltpu.SemaphoreType.DMA((2, 8, N)),
            pltpu.SemaphoreType.DMA((E,)),
            pltpu.SemaphoreType.DMA((E,)),
            pltpu.SemaphoreType.DMA((E,)),
            pltpu.SemaphoreType.DMA((E,)),
        ],
        compiler_params=pltpu.CompilerParams(
            collective_id=0, has_side_effects=True, vmem_limit_bytes=48 * 1024 * 1024
        ),
    )(w, tokens[0].T, expert_ids[0].T, slot_pos[0].T, smooth, act_grad[0])
    dw = dw[:, :KC, :HID].transpose(1, 0, 2)
    return dtok.T[None], dw


def solution(mesh):
    return jax.shard_map(
        on_device,
        mesh=mesh,
        in_specs=(
            P("dp", "ep", None),
            P("dp", "ep", None),
            P("dp", "ep", None),
            P(),
            P("dp", None, "ep"),
            P("dp", None, "ep"),
        ),
        out_specs=(P("dp", "ep", None), P("dp", None, "ep")),
        check_vma=False,
    )
```

```python
import functools

import jax
import jax.numpy as jnp
from jax import lax
from jax.experimental import pallas as pl
from jax.experimental.pallas import tpu as pltpu
from jax.sharding import PartitionSpec as P

MESH = pl.DeviceIdType.MESH
F32 = jnp.float32
BF16 = jnp.bfloat16
ALPHA = 1.702
Z = 16
E = 32
SHARE = 8
SLOT = 5
ROWS = 160
D = 2880
KC = 180
KP = 184
CH = 1024
HID = 360
HP = 384
WIDE = 1024
BLK = 16
THIRDS = ((0, 1024), (1024, 1024), (2048, 832))
C4, C5, USED = 720, 900, 1020
SUBS = ((0, 368), (368, 352), (720, 144), (864, 160))
BACK = ((0, 352), (352, 368), (720, 144), (864, 160))
N = len(SUBS)
FAR = (0, 2)


def mm(a, b):
    return jnp.dot(a, b, preferred_element_type=F32)


def mm_nt(a, b):
    return lax.dot_general(a, b, (((1,), (1,)), ((), ())), preferred_element_type=F32)


def mm_tn(a, b):
    return lax.dot_general(a, b, (((0,), (0,)), ((), ())), preferred_element_type=F32)


def kernel(
    w_ref, tok_ref, ids_ref, pos_ref, smooth_ref, act_ref,
    dw_ref, dtok_ref,
    tok_vm, tok_sem, wbuf, tsend, trecv, rows32, d32, sct, scy, scz, fcol, acc, gall, cbuf, rsend, rrecv, bthird, psend, precv, actc,
    ag_ss, ag_rs, rs_ss, rs_rs, t_ss, t_rs, p_ss, p_rs,
):
    z = lax.axis_index("dp")
    me = lax.axis_index("ep")
    right, left = lax.rem(z + 1, Z), lax.rem(z + Z - 1, Z)
    group = me // SHARE
    sides = (right, left)

    barrier = pltpu.get_barrier_semaphore()
    for side in sides:
        pl.semaphore_signal(barrier, inc=1, device_id={"dp": side}, device_id_type=MESH)

    @pl.loop(1, E)
    def _(k):
        pl.semaphore_signal(
            barrier, inc=1, device_id={"ep": lax.rem(me + k, E)}, device_id_type=MESH
        )

    tok_load = pltpu.make_async_copy(tok_ref, tok_vm, tok_sem)
    tok_load.start()

    def lanes(rows, low, high):
        lane = lax.broadcasted_iota(jnp.int32, (rows, 128), 1)
        return (lane >= low) & (lane < high)

    def roll(x, shift):
        return pltpu.roll(x, shift, 1)

    def own_chunk():
        for u in range(2):
            for half in range(2):
                at = half * 2 * KC + u * KC
                piece = w_ref[u, :, half * 128 : half * 128 + 128].astype(F32)
                cbuf[0, at : at + KC] = piece[0:KC]
        gate = w_ref[0, :, 256:384].astype(F32)
        up = w_ref[1, :, 256:384].astype(F32)
        cbuf[0, C4:C5] = jnp.where(lanes(KP, 0, 104), gate, roll(up, 104))[0:KC]
        for at in range(2):
            cbuf[at, USED:CH] = jnp.zeros((CH - USED, 128), F32)
        cbuf[0, C5:USED] = jnp.where(lanes(120, 0, 80), roll(up[0:120], 104), 0.0)
        low = up[120:180]
        cbuf[0, C5 : C5 + 60] = cbuf[0, C5 : C5 + 60] + jnp.where(
            lanes(60, 80, 128), roll(low, 56), 0.0
        )
        cbuf[0, C5 + 60 : USED] = cbuf[0, C5 + 60 : USED] + jnp.where(
            lanes(60, 80, 112), roll(low, 8), 0.0
        )
        wbuf[z] = cbuf[0].astype(BF16)

    own_chunk()
    pl.semaphore_wait(barrier, E + 1)

    def far(way, sub):
        return (sub in FAR) == (way == 0)

    def ag_copy(s, way, sub, owner):
        first, count = SUBS[sub]
        part = wbuf.at[owner, pl.ds(first, count)]
        return pltpu.make_async_remote_copy(
            src_ref=part, dst_ref=part,
            send_sem=ag_ss.at[way, s, sub], recv_sem=ag_rs.at[way, s, sub],
            device_id={"dp": sides[way]}, device_id_type=MESH,
        )

    def ag_send(s, way, sub):
        owner = lax.rem(z + Z - s, Z) if way == 0 else lax.rem(z + s, Z)
        return ag_copy(s, way, sub, owner)

    def ag_recv(s, way, sub):
        owner = lax.rem(z + Z - 1 - s, Z) if way == 0 else lax.rem(z + 1 + s, Z)
        return ag_copy(s, way, sub, owner)

    def ag_sent(s):
        for sub in range(N):
            for way in range(2):
                if s < 7 or far(way, sub):
                    ag_send(s, way, sub).wait_send()

    for sub in range(N):
        for way in range(2):
            ag_send(0, way, sub).start()

    def match_rows(count, shift):
        row = lax.broadcasted_iota(jnp.int32, (count, 128), 0)
        g = row >> shift
        j = row & (BLK - 1)
        slot = (j * 11) >> 5
        third = j - 3 * slot
        hit = jnp.zeros((count, 128), jnp.bool_)
        for k in range(4):
            hit = hit | ((ids_ref[k : k + 1, :] == g) & (pos_ref[k : k + 1, :] == slot))
        return [
            jnp.where(hit & (third == t), 1.0, 0.0).astype(BF16) for t in range(3)
        ]

    tok_load.wait()
    sel = match_rows(4 * BLK, 4)
    for t, (first, count) in enumerate(THIRDS):
        rows = mm_nt(sel[t], tok_vm[first : first + count, :])
        if t == 0:
            rows32[...] = rows
        else:
            rows32[:, 0:count] = rows32[:, 0:count] + rows
    for g in range(4):
        tsend[g] = rows32[g * BLK : (g + 1) * BLK, :].astype(BF16)

    def t_copy(peer, block, slot_at, peer_sem):
        return pltpu.make_async_remote_copy(
            src_ref=tsend.at[block], dst_ref=trecv.at[slot_at],
            send_sem=t_ss.at[peer], recv_sem=t_rs.at[peer_sem],
            device_id={"ep": peer}, device_id_type=MESH,
        )

    @pl.loop(1, E)
    def _(k):
        peer = lax.rem(me + k, E)
        t_copy(peer, peer // SHARE, me, me).start()

    trecv[me] = tsend[group]

    def place_rows(t, tall, first=0, count=E * BLK):
        shape = (count, ROWS) if tall else (ROWS, count)
        wide = lax.broadcasted_iota(jnp.int32, shape, 0 if tall else 1) + first
        r = lax.broadcasted_iota(jnp.int32, shape, 1 if tall else 0)
        s = (r * 205) >> 10
        return jnp.where(wide == s * BLK + (r - SLOT * s) * 3 + t, 1.0, 0.0).astype(BF16)

    def t_sent():
        @pl.loop(1, E)
        def _(k):
            peer = lax.rem(me + k, E)
            t_copy(peer, peer // SHARE, me, me).wait_send()

    def t_wait():
        @pl.loop(1, E)
        def _(k):
            peer = lax.rem(me + E - k, E)
            t_copy(peer, 0, peer, peer).wait_recv()

    def factors():
        row = smooth_ref[pl.ds(group, 1), :]
        for first, count in THIRDS:
            piece = jnp.broadcast_to(row[:, first : first + count], (8, count))
            fcol[first : first + count, :] = piece.T
        acc[...] = jnp.zeros_like(acc)
        actc[...] = jnp.zeros_like(actc)
        actc[:, 0:104] = act_ref[:, 256:360].astype(F32)

    def dispatch(t):
        first, count = THIRDS[t]
        wide = trecv[...].reshape(E * BLK, WIDE)
        rows = mm(place_rows(t, False), wide[:, 0:count])
        factor = smooth_ref[pl.ds(group, 1), first : first + count]
        scaled = (rows / factor).astype(BF16).astype(F32)
        d32[first : first + count, :] = scaled.T
        if t == 2:
            d32[D : D + 64, :] = jnp.zeros((64, ROWS), F32)

    def chunks(low, high):
        for o in range(low, high):
            at = KC * o
            row = lax.broadcasted_iota(jnp.int32, (KP, ROWS), 0)
            sct[o] = jnp.where(row < KC, d32[at : at + KP, :], 0.0).astype(BF16)
            row = lax.broadcasted_iota(jnp.int32, (120, ROWS), 0)
            scy[o] = jnp.where(row < 60, d32[at + 120 : at + 240, :], 0.0).astype(BF16)
            scz[o] = jnp.where(row >= 60, d32[at + 60 : at + 180, :], 0.0).astype(BF16)

    def forward(o, part):
        if part < 2:
            first = 2 * KC * part
            pair = jnp.concatenate(
                [wbuf[o, first : first + KC], wbuf[o, first + KC : first + 2 * KC]], axis=1
            )
            at = 256 * part
            acc[:, at : at + 256] = acc[:, at : at + 256] + mm_tn(sct[o, 0:KC], pair)
        else:
            block = wbuf[o, C5:USED]
            acc[:, 512:640] = acc[:, 512:640] + mm_tn(sct[o, 0:KC], wbuf[o, C4:C5])
            acc[:, 640:768] = acc[:, 640:768] + mm_tn(sct[o, 0:120], block)
            acc[:, 768:896] = acc[:, 768:896] + mm_tn(scy[o], block)
            acc[:, 896:1024] = acc[:, 896:1024] + mm_tn(scz[o], block)

    def forward_at(*steps):
        for d in steps:
            for part in range(3):
                forward(lax.rem(z + Z + d, Z), part)

    def forward_pair(d, part):
        forward(lax.rem(z + Z + d, Z), part)
        forward(lax.rem(z + Z - d, Z), part)

    ag_tasks = {
        (1, 0): factors,
        (3, 1): lambda: (t_wait(), dispatch(0)),
        (3, 2): lambda: dispatch(1),
        (3, 3): lambda: dispatch(2),
        (4, 0): lambda: chunks(0, 4),
        (4, 1): lambda: chunks(4, 8),
        (4, 2): lambda: chunks(8, 12),
        (4, 3): lambda: chunks(12, 16),
        (5, 0): lambda: forward_at(0, 1),
        (5, 1): lambda: forward_at(-1, 2),
        (5, 2): lambda: forward_at(-2, 3),
        (5, 3): lambda: forward_at(-3, 4),
        (6, 0): lambda: forward_at(-4, 5),
        (6, 1): lambda: forward_at(-5),
        (6, 2): t_sent,
        (6, 3): lambda: forward_at(-6),
        (7, 0): lambda: (forward_pair(7, 0), forward(lax.rem(z + 6, Z), 0)),
        (7, 1): lambda: (forward_pair(7, 1), forward(lax.rem(z + 6, Z), 1)),
        (7, 2): lambda: forward(lax.rem(z + 6, Z), 2),
        (7, 3): lambda: forward_pair(7, 2),
    }
    for s in range(1, 8):
        for sub in range(N):
            for way in range(2):
                ag_recv(s - 1, way, sub).wait_recv()
                if s < 7 or far(way, sub):
                    ag_send(s, way, sub).start()
            ag_tasks.get((s, sub), lambda: None)()
        if s > 1:
            ag_sent(s - 2)

    def gradients(gate, up, c):
        q = 1.0 / (1.0 + jnp.exp(-ALPHA * gate))
        gg = c * (up + 1.0) * q * (1.0 + ALPHA * gate * (1.0 - q))
        return gg, c * gate * q

    def activate(part):
        at = 256 * part
        if part < 2:
            c = act_ref[:, 128 * part : 128 * part + 128].astype(F32)
            gg, gu = gradients(acc[:, at : at + 128], acc[:, at + 128 : at + 256], c)
            gall[:, at : at + 128] = gg.astype(BF16)
            gall[:, at + 128 : at + 256] = gu.astype(BF16)
            return
        gate = acc[:, 512:640]
        up = jnp.where(lanes(ROWS, 0, 24), roll(gate, 24), 0.0)
        up = jnp.where(lanes(ROWS, 24, 104), roll(acc[:, 640:768], 24), up)
        up = up + jnp.where(lanes(ROWS, 24, 72), roll(acc[:, 768:896], 72), 0.0)
        up = up + jnp.where(lanes(ROWS, 72, 104), roll(acc[:, 896:1024], 120), 0.0)
        gg, gu = gradients(gate, up, actc[...])
        turned = roll(gu, 104)
        gall[:, 512:640] = jnp.where(lanes(ROWS, 0, 104), gg, turned).astype(BF16)
        gall[:, 640:768] = jnp.where(lanes(ROWS, 0, 80), turned, 0.0).astype(BF16)
        gall[:, 768:896] = jnp.where(lanes(ROWS, 80, 128), roll(gu, 56), 0.0).astype(BF16)
        gall[:, 896:1024] = jnp.where(lanes(ROWS, 80, 112), roll(gu, 8), 0.0).astype(BF16)

    def term(o, part, at):
        if part < 2:
            pair = mm(sct[o], gall[:, 256 * part : 256 * part + 256])
            first = 2 * KC * part
            cbuf[at, first : first + KC] = pair[0:KC, 0:128]
            cbuf[at, first + KC : first + 2 * KC] = pair[0:KC, 128:256]
        else:
            cbuf[at, C4:C5] = mm(sct[o], gall[:, 512:640])[0:KC]
            cbuf[at, C5:USED] = (
                mm(sct[o, 0:120], gall[:, 640:768])
                + mm(scy[o], gall[:, 768:896])
                + mm(scz[o], gall[:, 896:1024])
            )

    def rs_copy(t, way, sub):
        first, count = BACK[sub]
        return pltpu.make_async_remote_copy(
            src_ref=rsend.at[way, t, pl.ds(first, count)],
            dst_ref=rrecv.at[way, t, pl.ds(first, count)],
            send_sem=rs_ss.at[way, t, sub], recv_sem=rs_rs.at[way, t, sub],
            device_id={"dp": sides[way]}, device_id_type=MESH,
        )

    def rs_send(t, way, sub, at, add):
        first, count = BACK[sub]
        value = cbuf[at, first : first + count]
        if add:
            rs_copy(t - 1, way, sub).wait_recv()
            value = value + rrecv[way, t - 1, first : first + count].astype(F32)
        rsend[way, t, first : first + count] = value.astype(BF16)
        rs_copy(t, way, sub).start()

    def rs_sent(t):
        for sub in range(N):
            for way in range(2):
                if t > 0 or far(way, sub):
                    rs_copy(t, way, sub).wait_send()

    def owner(t, way):
        return lax.rem(z + 8 - t + Z, Z) if way == 0 else lax.rem(z + 8 + t, Z)

    def turn(part, subs):
        opposite = lax.rem(z + 8, Z)
        for sub in subs:
            ag_recv(7, 0 if far(0, sub) else 1, sub).wait_recv()
        forward(opposite, part)
        activate(part)
        term(opposite, part, 0)
        for sub in subs:
            rs_send(0, 0 if far(0, sub) else 1, sub, 0, False)
        for way in range(2):
            if any(not far(way, sub) for sub in subs):
                if part == 1:
                    term(owner(1, way), 0, 1)
                term(owner(1, way), part, 1)
                for sub in subs:
                    if not far(way, sub):
                        rs_send(1, way, sub, 1, False)

    turn(0, (0,))
    turn(1, (1,))
    turn(2, (2, 3))

    def back(low, high):
        for o in range(low, high):
            pairs = jnp.concatenate(
                [wbuf[o, first : first + KC] for first in range(0, C5, KC)], axis=1
            )
            block = wbuf[o, C5:USED]
            at = KC * o
            d32[at : at + KC, :] = mm_nt(pairs, gall[:, 0:640])
            d32[at : at + 120, :] = d32[at : at + 120, :] + mm_nt(block, gall[:, 640:768])
            low_rows = mm_nt(block, gall[:, 768:896])
            high_rows = mm_nt(block, gall[:, 896:1024])
            d32[at + 120 : at + 180, :] = (
                d32[at + 120 : at + 180, :] + low_rows[0:60] + high_rows[60:120]
            )

    def unscale():
        for first, count in THIRDS:
            bthird[first : first + count, :] = (
                d32[first : first + count, :] / fcol[first : first + count, 0:1]
            ).astype(BF16)
        bthird[D : 3 * WIDE, :] = jnp.zeros((3 * WIDE - D, ROWS), BF16)

    def expand(half):
        first = half * (E // 2) * BLK
        total = None
        for t in range(3):
            place = place_rows(t, True, first, (E // 2) * BLK)
            rows = mm_nt(place, bthird[WIDE * t : WIDE * (t + 1), :])
            total = rows if total is None else total + rows
        at = half * (E // 2)
        psend[at : at + E // 2] = total.astype(BF16).reshape(E // 2, BLK, WIDE)

    def p_copy(peer, block, slot_at, peer_sem):
        return pltpu.make_async_remote_copy(
            src_ref=psend.at[block], dst_ref=precv.at[slot_at],
            send_sem=p_ss.at[peer], recv_sem=p_rs.at[peer_sem],
            device_id={"ep": peer}, device_id_type=MESH,
        )

    def p_start():
        @pl.loop(1, E)
        def _(k):
            peer = lax.rem(me + k, E)
            p_copy(peer, peer, me, me).start()

        precv[me] = psend[me]

    def p_sent():
        @pl.loop(1, E)
        def _(k):
            peer = lax.rem(me + k, E)
            p_copy(peer, peer, me, me).wait_send()

    def p_wait():
        @pl.loop(1, E)
        def _(k):
            peer = lax.rem(me + E - k, E)
            p_copy(peer, 0, peer, peer).wait_recv()

    def combine(t):
        first, count = THIRDS[t]
        flat = precv[...].reshape(E * BLK, WIDE)
        pick = match_rows(E * BLK, 7)[t]
        dtok_ref[first : first + count, :] = mm_tn(flat[:, 0:count], pick).astype(BF16)

    rs_tasks = {
        (1, 0): lambda: back(0, 2),
        (1, 1): lambda: back(2, 4),
        (1, 2): lambda: back(4, 6),
        (1, 3): lambda: back(6, 8),
        (2, 0): lambda: back(8, 10),
        (2, 1): lambda: back(10, 12),
        (2, 2): lambda: back(12, 14),
        (2, 3): lambda: back(14, 16),
        (3, 0): unscale,
        (3, 1): lambda: expand(0),
        (3, 2): lambda: expand(1),
        (3, 3): p_start,
        (6, 1): lambda: (p_wait(), combine(0)),
        (6, 2): lambda: combine(1),
        (6, 3): lambda: combine(2),
        (7, 0): p_sent,
    }
    for t in range(1, 8):
        for sub in range(N):
            for way in range(2):
                if t == 1 and not far(way, sub):
                    continue
                if t == 1 and sub == 1:
                    term(owner(t, way), 0, way)
                if sub < 3:
                    term(owner(t, way), sub, way)
                elif t == 1:
                    term(owner(t, way), 2, way)
                rs_send(t, way, sub, way, True)
            rs_tasks.get((t, sub), lambda: None)()
        if t < 3:
            ag_sent(5 + t)
        else:
            rs_sent(t - 3)
    for sub in range(N):
        first, count = BACK[sub]
        if sub < 3:
            term(z, sub, 0)
        value = cbuf[0, first : first + count]
        for way in range(2):
            rs_copy(7, way, sub).wait_recv()
            value = value + rrecv[way, 7, first : first + count].astype(F32)
        cbuf[1, first : first + count] = value
        if sub == 1:
            for u in range(2):
                for half in range(2):
                    at = half * 2 * KC + u * KC
                    dw_ref[u, 0:KC, 128 * half : 128 * half + 128] = cbuf[1, at : at + KC]
    mixed = cbuf[1, C4:C5]
    dw_ref[0, 0:KC, 256:384] = mixed
    dw_ref[1, 0:KC, 256:384] = jnp.where(lanes(KC, 0, 24), roll(mixed, 24), 0.0)
    dw_ref[1, 0:120, 256:384] = jnp.where(
        lanes(120, 24, 104), roll(cbuf[1, C5:USED], 24), dw_ref[1, 0:120, 256:384]
    )
    low = jnp.where(lanes(60, 24, 72), roll(cbuf[1, C5 : C5 + 60], 72), 0.0)
    high = jnp.where(lanes(60, 72, 104), roll(cbuf[1, C5 + 60 : USED], 120), 0.0)
    dw_ref[1, 120:180, 256:384] = dw_ref[1, 120:180, 256:384] + low + high

    for t in range(5, 8):
        rs_sent(t)


def on_device(tokens, expert_ids, slot_pos, smooth, smoothed_weight, act_grad):
    w = jnp.transpose(smoothed_weight, (1, 0, 2))
    w = jnp.pad(w, ((0, 0), (0, KP - KC), (0, HP - HID)))
    vmem = pl.BlockSpec(memory_space=pltpu.VMEM)
    dw, dtok = pl.pallas_call(
        kernel,
        out_shape=(
            jax.ShapeDtypeStruct((2, KP, HP), F32),
            jax.ShapeDtypeStruct((D, 128), BF16),
        ),
        in_specs=[vmem, pl.BlockSpec(memory_space=pl.ANY)] + [vmem] * 4,
        out_specs=(vmem, vmem),
        scratch_shapes=[
            pltpu.VMEM((D, 128), BF16),
            pltpu.SemaphoreType.DMA,
            pltpu.VMEM((Z, CH, 128), BF16),
            pltpu.VMEM((4, BLK, WIDE), BF16),
            pltpu.VMEM((E, BLK, WIDE), BF16),
            pltpu.VMEM((4 * BLK, WIDE), F32),
            pltpu.VMEM((D + 64, ROWS), F32),
            pltpu.VMEM((Z, KP, ROWS), BF16),
            pltpu.VMEM((Z, 120, ROWS), BF16),
            pltpu.VMEM((Z, 120, ROWS), BF16),
            pltpu.VMEM((D, 8), F32),
            pltpu.VMEM((ROWS, 1024), F32),
            pltpu.VMEM((ROWS, 1024), BF16),
            pltpu.VMEM((2, CH, 128), F32),
            pltpu.VMEM((2, 8, CH, 128), BF16),
            pltpu.VMEM((2, 8, CH, 128), BF16),
            pltpu.VMEM((3 * WIDE, ROWS), BF16),
            pltpu.VMEM((E, BLK, WIDE), BF16),
            pltpu.VMEM((E, BLK, WIDE), BF16),
            pltpu.VMEM((ROWS, 128), F32),
            pltpu.SemaphoreType.DMA((2, 8, N)),
            pltpu.SemaphoreType.DMA((2, 8, N)),
            pltpu.SemaphoreType.DMA((2, 8, N)),
            pltpu.SemaphoreType.DMA((2, 8, N)),
            pltpu.SemaphoreType.DMA((E,)),
            pltpu.SemaphoreType.DMA((E,)),
            pltpu.SemaphoreType.DMA((E,)),
            pltpu.SemaphoreType.DMA((E,)),
        ],
        compiler_params=pltpu.CompilerParams(
            collective_id=0, has_side_effects=True, vmem_limit_bytes=48 * 1024 * 1024
        ),
    )(w, tokens[0].T, expert_ids[0].T, slot_pos[0].T, smooth, act_grad[0])
    dw = dw[:, :KC, :HID].transpose(1, 0, 2)
    return dtok.T[None], dw


def solution(mesh):
    return jax.shard_map(
        on_device,
        mesh=mesh,
        in_specs=(
            P("dp", "ep", None),
            P("dp", "ep", None),
            P("dp", "ep", None),
            P(),
            P("dp", None, "ep"),
            P("dp", None, "ep"),
        ),
        out_specs=(P("dp", "ep", None), P("dp", None, "ep")),
        check_vma=False,
    )
```

```python
import functools

import jax
import jax.numpy as jnp
from jax import lax
from jax.experimental import pallas as pl
from jax.experimental.pallas import tpu as pltpu
from jax.sharding import PartitionSpec as P

MESH = pl.DeviceIdType.MESH
F32 = jnp.float32
BF16 = jnp.bfloat16
ALPHA = 1.702
Z = 16
E = 32
SHARE = 8
SLOT = 5
ROWS = 160
D = 2880
KC = 180
KP = 184
CH = 1024
HID = 360
HP = 384
WIDE = 1024
BLK = 16
THIRDS = ((0, 1024), (1024, 1024), (2048, 832))
C4, C5, USED = 720, 900, 1020
SUBS = ((0, 368), (368, 352), (720, 144), (864, 160))
BACK = ((0, 352), (352, 368), (720, 144), (864, 160))
N = len(SUBS)
FAR = (0, 2)


def mm(a, b):
    return jnp.dot(a, b, preferred_element_type=F32)


def mm_nt(a, b):
    return lax.dot_general(a, b, (((1,), (1,)), ((), ())), preferred_element_type=F32)


def mm_tn(a, b):
    return lax.dot_general(a, b, (((0,), (0,)), ((), ())), preferred_element_type=F32)


def kernel(
    w_ref, tok_ref, ids_ref, pos_ref, smooth_ref, act_ref,
    dw_ref, dtok_ref,
    tok_vm, tok_sem, wbuf, tsend, trecv, rows32, d32, sct, scy, scz, fcol, acc, gall, cbuf, rsend, rrecv, bthird, psend, precv, actc,
    ag_ss, ag_rs, rs_ss, rs_rs, t_ss, t_rs, p_ss, p_rs,
):
    z = lax.axis_index("dp")
    me = lax.axis_index("ep")
    right, left = lax.rem(z + 1, Z), lax.rem(z + Z - 1, Z)
    group = me // SHARE
    sides = (right, left)

    barrier = pltpu.get_barrier_semaphore()
    for side in sides:
        pl.semaphore_signal(barrier, inc=1, device_id={"dp": side}, device_id_type=MESH)

    @pl.loop(1, E)
    def _(k):
        pl.semaphore_signal(
            barrier, inc=1, device_id={"ep": lax.rem(me + k, E)}, device_id_type=MESH
        )

    tok_load = pltpu.make_async_copy(tok_ref, tok_vm, tok_sem)
    tok_load.start()

    def lanes(rows, low, high):
        lane = lax.broadcasted_iota(jnp.int32, (rows, 128), 1)
        return (lane >= low) & (lane < high)

    def roll(x, shift):
        return pltpu.roll(x, shift, 1)

    def own_chunk():
        for u in range(2):
            for half in range(2):
                at = half * 2 * KC + u * KC
                piece = w_ref[u, :, half * 128 : half * 128 + 128].astype(F32)
                cbuf[0, at : at + KC] = piece[0:KC]
        gate = w_ref[0, :, 256:384].astype(F32)
        up = w_ref[1, :, 256:384].astype(F32)
        cbuf[0, C4:C5] = jnp.where(lanes(KP, 0, 104), gate, roll(up, 104))[0:KC]
        for at in range(2):
            cbuf[at, USED:CH] = jnp.zeros((CH - USED, 128), F32)
        cbuf[0, C5:USED] = jnp.where(lanes(120, 0, 80), roll(up[0:120], 104), 0.0)
        low = up[120:180]
        cbuf[0, C5 : C5 + 60] = cbuf[0, C5 : C5 + 60] + jnp.where(
            lanes(60, 80, 128), roll(low, 56), 0.0
        )
        cbuf[0, C5 + 60 : USED] = cbuf[0, C5 + 60 : USED] + jnp.where(
            lanes(60, 80, 112), roll(low, 8), 0.0
        )
        wbuf[z] = cbuf[0].astype(BF16)

    own_chunk()
    pl.semaphore_wait(barrier, E + 1)

    def far(way, sub):
        return (sub in FAR) == (way == 0)

    def ag_copy(s, way, sub, owner):
        first, count = SUBS[sub]
        part = wbuf.at[owner, pl.ds(first, count)]
        return pltpu.make_async_remote_copy(
            src_ref=part, dst_ref=part,
            send_sem=ag_ss.at[way, s, sub], recv_sem=ag_rs.at[way, s, sub],
            device_id={"dp": sides[way]}, device_id_type=MESH,
        )

    def ag_send(s, way, sub):
        owner = lax.rem(z + Z - s, Z) if way == 0 else lax.rem(z + s, Z)
        return ag_copy(s, way, sub, owner)

    def ag_recv(s, way, sub):
        owner = lax.rem(z + Z - 1 - s, Z) if way == 0 else lax.rem(z + 1 + s, Z)
        return ag_copy(s, way, sub, owner)

    def ag_sent(s):
        for sub in range(N):
            for way in range(2):
                if s < 7 or far(way, sub):
                    ag_send(s, way, sub).wait_send()

    for sub in range(N):
        for way in range(2):
            ag_send(0, way, sub).start()

    def match_rows(count, shift):
        row = lax.broadcasted_iota(jnp.int32, (count, 128), 0)
        g = row >> shift
        j = row & (BLK - 1)
        slot = (j * 11) >> 5
        third = j - 3 * slot
        hit = jnp.zeros((count, 128), jnp.bool_)
        for k in range(4):
            hit = hit | ((ids_ref[k : k + 1, :] == g) & (pos_ref[k : k + 1, :] == slot))
        return [
            jnp.where(hit & (third == t), 1.0, 0.0).astype(BF16) for t in range(3)
        ]

    tok_load.wait()
    sel = match_rows(4 * BLK, 4)
    for t, (first, count) in enumerate(THIRDS):
        rows = mm_nt(sel[t], tok_vm[first : first + count, :])
        if t == 0:
            rows32[...] = rows
        else:
            rows32[:, 0:count] = rows32[:, 0:count] + rows
    for g in range(4):
        tsend[g] = rows32[g * BLK : (g + 1) * BLK, :].astype(BF16)

    def t_copy(peer, block, slot_at, peer_sem):
        return pltpu.make_async_remote_copy(
            src_ref=tsend.at[block], dst_ref=trecv.at[slot_at],
            send_sem=t_ss.at[peer], recv_sem=t_rs.at[peer_sem],
            device_id={"ep": peer}, device_id_type=MESH,
        )

    @pl.loop(1, E)
    def _(k):
        peer = lax.rem(me + k, E)
        t_copy(peer, peer // SHARE, me, me).start()

    trecv[me] = tsend[group]

    def place_rows(t, tall, first=0, count=E * BLK):
        shape = (count, ROWS) if tall else (ROWS, count)
        wide = lax.broadcasted_iota(jnp.int32, shape, 0 if tall else 1) + first
        r = lax.broadcasted_iota(jnp.int32, shape, 1 if tall else 0)
        s = (r * 205) >> 10
        return jnp.where(wide == s * BLK + (r - SLOT * s) * 3 + t, 1.0, 0.0).astype(BF16)

    def t_sent():
        @pl.loop(1, E)
        def _(k):
            peer = lax.rem(me + k, E)
            t_copy(peer, peer // SHARE, me, me).wait_send()

    def t_wait():
        @pl.loop(1, E)
        def _(k):
            peer = lax.rem(me + E - k, E)
            t_copy(peer, 0, peer, peer).wait_recv()

    def factors():
        row = smooth_ref[pl.ds(group, 1), :]
        for first, count in THIRDS:
            piece = jnp.broadcast_to(row[:, first : first + count], (8, count))
            fcol[first : first + count, :] = piece.T
        acc[...] = jnp.zeros_like(acc)
        actc[...] = jnp.zeros_like(actc)
        actc[:, 0:104] = act_ref[:, 256:360].astype(F32)

    def dispatch(t):
        first, count = THIRDS[t]
        wide = trecv[...].reshape(E * BLK, WIDE)
        rows = mm(place_rows(t, False), wide[:, 0:count])
        factor = smooth_ref[pl.ds(group, 1), first : first + count]
        scaled = (rows / factor).astype(BF16).astype(F32)
        d32[first : first + count, :] = scaled.T
        if t == 2:
            d32[D : D + 64, :] = jnp.zeros((64, ROWS), F32)

    def chunks(low, high):
        for o in range(low, high):
            at = KC * o
            row = lax.broadcasted_iota(jnp.int32, (KP, ROWS), 0)
            sct[o] = jnp.where(row < KC, d32[at : at + KP, :], 0.0).astype(BF16)
            row = lax.broadcasted_iota(jnp.int32, (120, ROWS), 0)
            scy[o] = jnp.where(row < 60, d32[at + 120 : at + 240, :], 0.0).astype(BF16)
            scz[o] = jnp.where(row >= 60, d32[at + 60 : at + 180, :], 0.0).astype(BF16)

    def forward(o, part):
        if part < 2:
            first = 2 * KC * part
            pair = jnp.concatenate(
                [wbuf[o, first : first + KC], wbuf[o, first + KC : first + 2 * KC]], axis=1
            )
            at = 256 * part
            acc[:, at : at + 256] = acc[:, at : at + 256] + mm_tn(sct[o, 0:KC], pair)
        else:
            block = wbuf[o, C5:USED]
            acc[:, 512:640] = acc[:, 512:640] + mm_tn(sct[o, 0:KC], wbuf[o, C4:C5])
            acc[:, 640:768] = acc[:, 640:768] + mm_tn(sct[o, 0:120], block)
            acc[:, 768:896] = acc[:, 768:896] + mm_tn(scy[o], block)
            acc[:, 896:1024] = acc[:, 896:1024] + mm_tn(scz[o], block)

    def forward_at(*steps):
        for d in steps:
            for part in range(3):
                forward(lax.rem(z + Z + d, Z), part)

    def forward_pair(d, part):
        forward(lax.rem(z + Z + d, Z), part)
        forward(lax.rem(z + Z - d, Z), part)

    ag_tasks = {
        (1, 0): factors,
        (3, 1): lambda: (t_wait(), dispatch(0)),
        (3, 2): lambda: dispatch(1),
        (3, 3): lambda: dispatch(2),
        (4, 0): lambda: chunks(0, 4),
        (4, 1): lambda: chunks(4, 8),
        (4, 2): lambda: chunks(8, 12),
        (4, 3): lambda: chunks(12, 16),
        (5, 0): lambda: forward_at(0, 1),
        (5, 1): lambda: forward_at(-1, 2),
        (5, 2): lambda: forward_at(-2, 3),
        (5, 3): lambda: forward_at(-3, 4),
        (6, 0): lambda: forward_at(-4, 5),
        (6, 1): lambda: forward_at(-5),
        (6, 2): t_sent,
        (6, 3): lambda: forward_at(-6),
        (7, 0): lambda: (forward_pair(7, 0), forward(lax.rem(z + 6, Z), 0)),
        (7, 1): lambda: (forward_pair(7, 1), forward(lax.rem(z + 6, Z), 1)),
        (7, 2): lambda: forward(lax.rem(z + 6, Z), 2),
        (7, 3): lambda: forward_pair(7, 2),
    }
    for s in range(1, 8):
        for sub in range(N):
            for way in range(2):
                ag_recv(s - 1, way, sub).wait_recv()
                if s < 7 or far(way, sub):
                    ag_send(s, way, sub).start()
            ag_tasks.get((s, sub), lambda: None)()
        if s > 1:
            ag_sent(s - 2)

    def gradients(gate, up, c):
        q = 1.0 / (1.0 + jnp.exp(-ALPHA * gate))
        gg = c * (up + 1.0) * q * (1.0 + ALPHA * gate * (1.0 - q))
        return gg, c * gate * q

    def activate(part):
        at = 256 * part
        if part < 2:
            c = act_ref[:, 128 * part : 128 * part + 128].astype(F32)
            gg, gu = gradients(acc[:, at : at + 128], acc[:, at + 128 : at + 256], c)
            gall[:, at : at + 128] = gg.astype(BF16)
            gall[:, at + 128 : at + 256] = gu.astype(BF16)
            return
        gate = acc[:, 512:640]
        up = jnp.where(lanes(ROWS, 0, 24), roll(gate, 24), 0.0)
        up = jnp.where(lanes(ROWS, 24, 104), roll(acc[:, 640:768], 24), up)
        up = up + jnp.where(lanes(ROWS, 24, 72), roll(acc[:, 768:896], 72), 0.0)
        up = up + jnp.where(lanes(ROWS, 72, 104), roll(acc[:, 896:1024], 120), 0.0)
        gg, gu = gradients(gate, up, actc[...])
        turned = roll(gu, 104)
        gall[:, 512:640] = jnp.where(lanes(ROWS, 0, 104), gg, turned).astype(BF16)
        gall[:, 640:768] = jnp.where(lanes(ROWS, 0, 80), turned, 0.0).astype(BF16)
        gall[:, 768:896] = jnp.where(lanes(ROWS, 80, 128), roll(gu, 56), 0.0).astype(BF16)
        gall[:, 896:1024] = jnp.where(lanes(ROWS, 80, 112), roll(gu, 8), 0.0).astype(BF16)

    def term(o, part, at):
        if part < 2:
            pair = mm(sct[o], gall[:, 256 * part : 256 * part + 256])
            first = 2 * KC * part
            cbuf[at, first : first + KC] = pair[0:KC, 0:128]
            cbuf[at, first + KC : first + 2 * KC] = pair[0:KC, 128:256]
        else:
            cbuf[at, C4:C5] = mm(sct[o], gall[:, 512:640])[0:KC]
            cbuf[at, C5:USED] = (
                mm(sct[o, 0:120], gall[:, 640:768])
                + mm(scy[o], gall[:, 768:896])
                + mm(scz[o], gall[:, 896:1024])
            )

    def edge(o, at):
        cbuf[at, 340:360] = mm(sct[o, 160:KC], gall[:, 128:256])

    def rs_copy(t, way, sub):
        first, count = BACK[sub]
        return pltpu.make_async_remote_copy(
            src_ref=rsend.at[way, t, pl.ds(first, count)],
            dst_ref=rrecv.at[way, t, pl.ds(first, count)],
            send_sem=rs_ss.at[way, t, sub], recv_sem=rs_rs.at[way, t, sub],
            device_id={"dp": sides[way]}, device_id_type=MESH,
        )

    def rs_send(t, way, sub, at, add):
        first, count = BACK[sub]
        value = cbuf[at, first : first + count]
        if add:
            rs_copy(t - 1, way, sub).wait_recv()
            value = value + rrecv[way, t - 1, first : first + count].astype(F32)
        rsend[way, t, first : first + count] = value.astype(BF16)
        rs_copy(t, way, sub).start()

    def rs_sent(t):
        for sub in range(N):
            for way in range(2):
                if t > 0 or far(way, sub):
                    rs_copy(t, way, sub).wait_send()

    def owner(t, way):
        return lax.rem(z + 8 - t + Z, Z) if way == 0 else lax.rem(z + 8 + t, Z)

    def turn(part, subs):
        opposite = lax.rem(z + 8, Z)
        for sub in subs:
            ag_recv(7, 0 if far(0, sub) else 1, sub).wait_recv()
        forward(opposite, part)
        activate(part)
        term(opposite, part, 0)
        for sub in subs:
            rs_send(0, 0 if far(0, sub) else 1, sub, 0, False)
        for way in range(2):
            if any(not far(way, sub) for sub in subs):
                if part == 1:
                    edge(owner(1, way), 1)
                term(owner(1, way), part, 1)
                for sub in subs:
                    if not far(way, sub):
                        rs_send(1, way, sub, 1, False)

    turn(0, (0,))
    turn(1, (1,))
    turn(2, (2, 3))

    def back(low, high):
        for o in range(low, high):
            pairs = jnp.concatenate(
                [wbuf[o, first : first + KC] for first in range(0, C5, KC)], axis=1
            )
            block = wbuf[o, C5:USED]
            at = KC * o
            d32[at : at + KC, :] = mm_nt(pairs, gall[:, 0:640])
            d32[at : at + 120, :] = d32[at : at + 120, :] + mm_nt(block, gall[:, 640:768])
            low_rows = mm_nt(block, gall[:, 768:896])
            high_rows = mm_nt(block, gall[:, 896:1024])
            d32[at + 120 : at + 180, :] = (
                d32[at + 120 : at + 180, :] + low_rows[0:60] + high_rows[60:120]
            )

    def unscale():
        for first, count in THIRDS:
            bthird[first : first + count, :] = (
                d32[first : first + count, :] / fcol[first : first + count, 0:1]
            ).astype(BF16)
        bthird[D : 3 * WIDE, :] = jnp.zeros((3 * WIDE - D, ROWS), BF16)

    def expand(half):
        first = half * (E // 2) * BLK
        total = None
        for t in range(3):
            place = place_rows(t, True, first, (E // 2) * BLK)
            rows = mm_nt(place, bthird[WIDE * t : WIDE * (t + 1), :])
            total = rows if total is None else total + rows
        at = half * (E // 2)
        psend[at : at + E // 2] = total.astype(BF16).reshape(E // 2, BLK, WIDE)

    def p_copy(peer, block, slot_at, peer_sem):
        return pltpu.make_async_remote_copy(
            src_ref=psend.at[block], dst_ref=precv.at[slot_at],
            send_sem=p_ss.at[peer], recv_sem=p_rs.at[peer_sem],
            device_id={"ep": peer}, device_id_type=MESH,
        )

    def p_start():
        @pl.loop(1, E)
        def _(k):
            peer = lax.rem(me + k, E)
            p_copy(peer, peer, me, me).start()

        precv[me] = psend[me]

    def p_sent():
        @pl.loop(1, E)
        def _(k):
            peer = lax.rem(me + k, E)
            p_copy(peer, peer, me, me).wait_send()

    def p_wait():
        @pl.loop(1, E)
        def _(k):
            peer = lax.rem(me + E - k, E)
            p_copy(peer, 0, peer, peer).wait_recv()

    def combine(t):
        first, count = THIRDS[t]
        flat = precv[...].reshape(E * BLK, WIDE)
        pick = match_rows(E * BLK, 7)[t]
        dtok_ref[first : first + count, :] = mm_tn(flat[:, 0:count], pick).astype(BF16)

    rs_tasks = {
        (1, 0): lambda: back(0, 2),
        (1, 1): lambda: back(2, 4),
        (1, 2): lambda: back(4, 6),
        (1, 3): lambda: back(6, 8),
        (2, 0): lambda: back(8, 10),
        (2, 1): lambda: back(10, 12),
        (2, 2): lambda: back(12, 14),
        (2, 3): lambda: back(14, 16),
        (3, 0): unscale,
        (3, 1): lambda: expand(0),
        (3, 2): lambda: expand(1),
        (3, 3): p_start,
        (6, 1): lambda: (p_wait(), combine(0)),
        (6, 2): lambda: combine(1),
        (6, 3): lambda: combine(2),
        (7, 0): p_sent,
    }
    for t in range(1, 8):
        for sub in range(N):
            for way in range(2):
                if t == 1 and not far(way, sub):
                    continue
                if t == 1 and sub == 1:
                    edge(owner(t, way), way)
                if sub < 3:
                    term(owner(t, way), sub, way)
                elif t == 1:
                    term(owner(t, way), 2, way)
                rs_send(t, way, sub, way, True)
            rs_tasks.get((t, sub), lambda: None)()
        if t < 3:
            ag_sent(5 + t)
        else:
            rs_sent(t - 3)
    for sub in range(N):
        first, count = BACK[sub]
        if sub < 3:
            term(z, sub, 0)
        value = cbuf[0, first : first + count]
        for way in range(2):
            rs_copy(7, way, sub).wait_recv()
            value = value + rrecv[way, 7, first : first + count].astype(F32)
        cbuf[1, first : first + count] = value
        if sub == 1:
            for u in range(2):
                for half in range(2):
                    at = half * 2 * KC + u * KC
                    dw_ref[u, 0:KC, 128 * half : 128 * half + 128] = cbuf[1, at : at + KC]
    mixed = cbuf[1, C4:C5]
    dw_ref[0, 0:KC, 256:384] = mixed
    dw_ref[1, 0:KC, 256:384] = jnp.where(lanes(KC, 0, 24), roll(mixed, 24), 0.0)
    dw_ref[1, 0:120, 256:384] = jnp.where(
        lanes(120, 24, 104), roll(cbuf[1, C5:USED], 24), dw_ref[1, 0:120, 256:384]
    )
    low = jnp.where(lanes(60, 24, 72), roll(cbuf[1, C5 : C5 + 60], 72), 0.0)
    high = jnp.where(lanes(60, 72, 104), roll(cbuf[1, C5 + 60 : USED], 120), 0.0)
    dw_ref[1, 120:180, 256:384] = dw_ref[1, 120:180, 256:384] + low + high

    for t in range(5, 8):
        rs_sent(t)


def on_device(tokens, expert_ids, slot_pos, smooth, smoothed_weight, act_grad):
    w = jnp.transpose(smoothed_weight, (1, 0, 2))
    w = jnp.pad(w, ((0, 0), (0, KP - KC), (0, HP - HID)))
    vmem = pl.BlockSpec(memory_space=pltpu.VMEM)
    dw, dtok = pl.pallas_call(
        kernel,
        out_shape=(
            jax.ShapeDtypeStruct((2, KP, HP), F32),
            jax.ShapeDtypeStruct((D, 128), BF16),
        ),
        in_specs=[vmem, pl.BlockSpec(memory_space=pl.ANY)] + [vmem] * 4,
        out_specs=(vmem, vmem),
        scratch_shapes=[
            pltpu.VMEM((D, 128), BF16),
            pltpu.SemaphoreType.DMA,
            pltpu.VMEM((Z, CH, 128), BF16),
            pltpu.VMEM((4, BLK, WIDE), BF16),
            pltpu.VMEM((E, BLK, WIDE), BF16),
            pltpu.VMEM((4 * BLK, WIDE), F32),
            pltpu.VMEM((D + 64, ROWS), F32),
            pltpu.VMEM((Z, KP, ROWS), BF16),
            pltpu.VMEM((Z, 120, ROWS), BF16),
            pltpu.VMEM((Z, 120, ROWS), BF16),
            pltpu.VMEM((D, 8), F32),
            pltpu.VMEM((ROWS, 1024), F32),
            pltpu.VMEM((ROWS, 1024), BF16),
            pltpu.VMEM((2, CH, 128), F32),
            pltpu.VMEM((2, 8, CH, 128), BF16),
            pltpu.VMEM((2, 8, CH, 128), BF16),
            pltpu.VMEM((3 * WIDE, ROWS), BF16),
            pltpu.VMEM((E, BLK, WIDE), BF16),
            pltpu.VMEM((E, BLK, WIDE), BF16),
            pltpu.VMEM((ROWS, 128), F32),
            pltpu.SemaphoreType.DMA((2, 8, N)),
            pltpu.SemaphoreType.DMA((2, 8, N)),
            pltpu.SemaphoreType.DMA((2, 8, N)),
            pltpu.SemaphoreType.DMA((2, 8, N)),
            pltpu.SemaphoreType.DMA((E,)),
            pltpu.SemaphoreType.DMA((E,)),
            pltpu.SemaphoreType.DMA((E,)),
            pltpu.SemaphoreType.DMA((E,)),
        ],
        compiler_params=pltpu.CompilerParams(
            collective_id=0, has_side_effects=True, vmem_limit_bytes=48 * 1024 * 1024
        ),
    )(w, tokens[0].T, expert_ids[0].T, slot_pos[0].T, smooth, act_grad[0])
    dw = dw[:, :KC, :HID].transpose(1, 0, 2)
    return dtok.T[None], dw


def solution(mesh):
    return jax.shard_map(
        on_device,
        mesh=mesh,
        in_specs=(
            P("dp", "ep", None),
            P("dp", "ep", None),
            P("dp", "ep", None),
            P(),
            P("dp", None, "ep"),
            P("dp", None, "ep"),
        ),
        out_specs=(P("dp", "ep", None), P("dp", None, "ep")),
        check_vma=False,
    )
```
